256 devices in a mesh: dp: 8 (over x, y_hi), tensor: 32 (over y_lo, z, core).
Axes of the slice: x: 4, y: 4 (y_hi: 2, y_lo: 2; y = y_hi * 2 + y_lo), z: 8, core: 2. Of those that a mesh axis runs over, the one named last changes fastest.
Arguments:
- tokens: bfloat16 [512, 16384], P('tensor', 'dp'), may hold values from -6 to 6
- gate_codes: int32 [4096, 53248], P('dp', 'tensor'), may hold values from 0 to 4095
- gate_scales: bfloat16 [128, 53248], P('dp', 'tensor'), may hold values from 0.00093460083 to 0.0078125
- up_codes: int32 [4096, 53248], P('dp', 'tensor'), may hold values from 0 to 4095
- up_scales: bfloat16 [128, 53248], P('dp', 'tensor'), may hold values from 0.00093460083 to 0.0078125
- down_codes: int32 [13312, 16384], P('tensor', 'dp'), may hold values from 0 to 4095
- down_scales: bfloat16 [416, 16384], P('tensor', 'dp'), may hold values from 0.0005187988 to 0.004333496
- flip_signs: int32 [53248], P('tensor'), may hold values from 0 to 1
Outputs:
- ffn_out: bfloat16 [512, 16384], P('tensor', 'dp')
The draws below stay inside these ranges and needn't reach their ends.
Inputs may be any that keep to these rules, and one draw needn't show every extreme that they name: `gate_codes`: each word holds four 3-bit codes: bits 3 j to 3 j + 2 that of row 4 i + j. `up_codes`: each word holds four 3-bit codes: bits 3 j to 3 j + 2 that of row 4 i + j. `down_codes`: each word holds four 3-bit codes: bits 3 j to 3 j + 2 that of hidden unit 4 i + j. `flip_signs`: 1 stands for plus one, 0 for minus one.
All inputs are finite; a program needn't handle non-finite values.
Results may differ from the reference program's by a relative error of at most 0.04.
Values may be sent and summed in bfloat16 or wider, within the bound.
A program may use at most 128 MiB of HBM per device.

```python
import math
import jax
import jax.numpy as jnp
import numpy as np
from jax import lax

D = 16384
FF = 53248
HG = 32
KB = 52
BLK = 32
GQ = 128
TOKENS = 512
N_DP = 8
N_TENSOR = 32


def with_ends(entries, key, low, largest):
    longest = entries.shape.index(max(entries.shape))
    spots = []
    for shift in (0, 1):
        where = [jax.random.randint(jax.random.fold_in(key, axis), (), 0, length) for axis, length in enumerate(entries.shape)]
        where[longest] = (where[longest] + shift) % entries.shape[longest]
        spots.append(tuple(where))
    return entries.at[spots[0]].set(low).at[spots[1]].set(largest)


def block_scale(stream_key, extent, split, smallest, largest):
    factor_of, own = 1.0, jax.random.fold_in(stream_key, 6)
    for axis_at, shards_of in split:
        draws = jnp.exp(jax.random.uniform(jax.random.fold_in(own, axis_at), (shards_of,), jnp.float32, smallest / len(split), largest / len(split)))
        factor_of = factor_of * jnp.repeat(draws, extent[axis_at] // shards_of).reshape([-1 if axis == axis_at else 1 for axis in range(len(extent))])
    return factor_of


def normal_values(key, shape, deviation, most, cuts=(), kind=jnp.bfloat16):
    values = deviation * jax.random.normal(key, shape, jnp.float32)
    if cuts:
        values = values * block_scale(key, shape, cuts, -0.22, 0.18)
    return jnp.clip(values, -most, most).astype(kind)


def setup_inputs(seed: int = 0) -> dict:
    seeds = jax.random.split(jax.random.key(seed), 9)
    return {
        "tokens": normal_values(seeds[0], (TOKENS, D), 1.0, 6.0, ((0, 32), (1, 8))),
        "gate_codes": with_ends(jax.random.randint(seeds[1], (D // 4, FF), 0, 4096), jax.random.fold_in(seeds[1], 1), 0, 4095).astype(jnp.int32),
        "gate_scales": jnp.clip(jnp.exp(math.log(0.0078125) - 2.1233608 * jax.random.uniform(seeds[2], (D // GQ, FF), jnp.float32) ** block_scale(seeds[2], (D // GQ, FF), ((0, 8), (1, 32)), -0.2, 0.2)), 0.00093460083, 0.0078125).astype(jnp.bfloat16),
        "up_codes": with_ends(jax.random.randint(seeds[3], (D // 4, FF), 0, 4096), jax.random.fold_in(seeds[3], 1), 0, 4095).astype(jnp.int32),
        "up_scales": jnp.clip(jnp.exp(math.log(0.0078125) - 2.1233608 * jax.random.uniform(seeds[4], (D // GQ, FF), jnp.float32) ** block_scale(seeds[4], (D // GQ, FF), ((0, 8), (1, 32)), -0.2, 0.2)), 0.00093460083, 0.0078125).astype(jnp.bfloat16),
        "down_codes": with_ends(jax.random.randint(seeds[5], (FF // 4, D), 0, 4096), jax.random.fold_in(seeds[5], 1), 0, 4095).astype(jnp.int32),
        "down_scales": jnp.clip(jnp.exp(math.log(0.004333496) - 2.1226137 * jax.random.uniform(seeds[6], (FF // GQ, D), jnp.float32) ** block_scale(seeds[6], (FF // GQ, D), ((0, 32), (1, 8)), -0.2, 0.2)), 0.0005187988, 0.004333496).astype(jnp.bfloat16),
        "flip_signs": with_ends(jax.random.randint(seeds[7], (FF,), 0, 2), jax.random.fold_in(seeds[7], 1), 0, 1).astype(jnp.int32),
    }


def paley_table():
    field_square = np.zeros(25, dtype=np.int64)
    for first_part in range(5):
        for second_part in range(5):
            if first_part == 0 and second_part == 0:
                continue
            real_part = (first_part * first_part + 2 * second_part * second_part) % 5
            root_part = (2 * first_part * second_part) % 5
            field_square[real_part + 5 * root_part] = 1
    character = np.where(field_square == 1, 1, -1)
    character[0] = 0
    jacobsthal = np.zeros((25, 25), dtype=np.int64)
    for left_item in range(25):
        for right_item in range(25):
            diff_real = (left_item % 5 - right_item % 5) % 5
            diff_root = (left_item // 5 - right_item // 5) % 5
            jacobsthal[left_item, right_item] = character[diff_real + 5 * diff_root]
    conference = np.zeros((26, 26), dtype=np.int64)
    conference[0, 1:] = 1
    conference[1:, 0] = 1
    conference[1:, 1:] = jacobsthal
    outer_part = np.array([[1, -1], [-1, -1]], dtype=np.int64)
    inner_part = np.array([[1, 1], [1, -1]], dtype=np.int64)
    return (np.kron(conference, outer_part) + np.kron(np.eye(26, dtype=np.int64), inner_part)).astype(np.float32)


def sylvester(order_size):
    position = jnp.arange(order_size, dtype=jnp.int32)
    parity = jnp.zeros((order_size, order_size), jnp.int32)
    for bit_place in range(max(order_size.bit_length() - 1, 0)):
        shared = jnp.right_shift(position[:, None], bit_place) & jnp.right_shift(position[None, :], bit_place)
        parity = parity + jnp.bitwise_and(shared, 1)
    return (1 - 2 * jnp.bitwise_and(parity, 1)).astype(jnp.float32)


def dequant(code_words, scales, group_size):
    shifts = 3 * jnp.arange(4, dtype=jnp.int32)
    nibbles = jnp.bitwise_and(jnp.right_shift(code_words[:, None, :], shifts[None, :, None]), 7)
    levels = nibbles.reshape(4 * code_words.shape[0], code_words.shape[1]) - 4
    spread = jnp.repeat(scales.astype(jnp.float32), group_size, axis=0)
    return (levels.astype(jnp.float32) * spread).astype(jnp.bfloat16)


def rounded_sum(partial_sum, running):
    rounded = lax.optimization_barrier(partial_sum.astype(jnp.bfloat16))
    return running + rounded.astype(jnp.float32)


def reference(tokens, gate_codes, gate_scales, up_codes, up_scales, down_codes, down_scales, flip_signs):
    rows_dp = D // N_DP
    gate_pre = jnp.zeros((TOKENS, FF), jnp.float32)
    up_pre = jnp.zeros((TOKENS, FF), jnp.float32)
    for dev_slot in range(N_DP):
        first_row = dev_slot * rows_dp
        part_in = tokens[:, first_row:first_row + rows_dp]
        gate_weight = dequant(gate_codes[first_row // 4:(first_row + rows_dp) // 4], gate_scales[first_row // GQ:(first_row + rows_dp) // GQ], GQ)
        gate_pre = rounded_sum(jnp.dot(part_in, gate_weight, preferred_element_type=jnp.float32), gate_pre)
        up_weight = dequant(up_codes[first_row // 4:(first_row + rows_dp) // 4], up_scales[first_row // GQ:(first_row + rows_dp) // GQ], GQ)
        up_pre = rounded_sum(jnp.dot(part_in, up_weight, preferred_element_type=jnp.float32), up_pre)
    hidden = (jax.nn.silu(gate_pre) * up_pre).astype(jnp.bfloat16)
    flipped = hidden.astype(jnp.float32) * (2 * flip_signs - 1).astype(jnp.float32)
    middle_table = jnp.asarray(paley_table(), dtype=jnp.float32)
    highest = lax.Precision.HIGHEST
    blocks = flipped.reshape(TOKENS, HG, KB, BLK)
    blocks = jnp.einsum('tgkb,bc->tgkc', blocks, sylvester(BLK), precision=highest)
    blocks = jnp.einsum('tgkc,kl->tglc', blocks, middle_table, precision=highest)
    blocks = jnp.einsum('tglc,gh->thlc', blocks, sylvester(HG), precision=highest)
    rotated = (blocks.reshape(TOKENS, FF) * (FF ** -0.5)).astype(jnp.bfloat16)
    rows_tp = FF // N_TENSOR
    output = jnp.zeros((TOKENS, D), jnp.float32)
    for dev_slot in range(N_TENSOR):
        first_row = dev_slot * rows_tp
        down_weight = dequant(down_codes[first_row // 4:(first_row + rows_tp) // 4], down_scales[first_row // GQ:(first_row + rows_tp) // GQ], GQ)
        output = rounded_sum(jnp.dot(rotated[:, first_row:first_row + rows_tp], down_weight, preferred_element_type=jnp.float32), output)
    return output.astype(jnp.bfloat16)
```

```python
import functools

import jax
import jax.numpy as jnp
import numpy as np
from jax import lax
from jax.experimental import pallas as pl
from jax.experimental.pallas import tpu as pltpu
from jax.sharding import PartitionSpec as P

FF = 53248
KB = 52
BLK = 32
MESH = pl.DeviceIdType.MESH
BF16 = jnp.bfloat16
F32 = jnp.float32
VMEM_LIMIT = 60 * 1024 * 1024


def paley_table():
    field_square = np.zeros(25, dtype=np.int64)
    for first_part in range(5):
        for second_part in range(5):
            if first_part == 0 and second_part == 0:
                continue
            real_part = (first_part * first_part + 2 * second_part * second_part) % 5
            root_part = 2 * first_part * second_part % 5
            field_square[real_part + 5 * root_part] = 1
    character = np.where(field_square == 1, 1, -1)
    character[0] = 0
    jacobsthal = np.zeros((25, 25), dtype=np.int64)
    for left_item in range(25):
        for right_item in range(25):
            diff_real = (left_item % 5 - right_item % 5) % 5
            diff_root = (left_item // 5 - right_item // 5) % 5
            jacobsthal[left_item, right_item] = character[diff_real + 5 * diff_root]
    conference = np.zeros((26, 26), dtype=np.int64)
    conference[0, 1:] = 1
    conference[1:, 0] = 1
    conference[1:, 1:] = jacobsthal
    outer_part = np.array([[1, -1], [-1, -1]], dtype=np.int64)
    inner_part = np.array([[1, 1], [1, -1]], dtype=np.int64)
    return np.kron(conference, outer_part) + np.kron(np.eye(26, dtype=np.int64), inner_part)


def sylvester_static(order_size):
    position = np.arange(order_size)
    parity = np.zeros((order_size, order_size), dtype=np.int64)
    for bit_place in range(max(order_size.bit_length() - 1, 0)):
        parity = parity + (position[:, None] >> bit_place & position[None, :] >> bit_place & 1)
    return 1 - 2 * (parity & 1)


def inner_table():
    table = np.kron(paley_table(), sylvester_static(BLK))
    order = (4 * np.arange(416)[None, :] + np.arange(4)[:, None]).reshape(-1)
    return table[:, order].astype(np.float32)


def remote(src, dst, send_sem, recv_sem, device):
    return pltpu.make_async_remote_copy(
        src_ref=src, dst_ref=dst, send_sem=send_sem, recv_sem=recv_sem, device_id=device, device_id_type=MESH
    )


def place():
    dp = lax.axis_index("dp")
    t = lax.axis_index("tensor")
    x, yh = lax.div(dp, 2), lax.rem(dp, 2)
    yl, z, core = lax.div(t, 16), lax.rem(lax.div(t, 2), 8), lax.rem(t, 2)
    return dp, t, x, yh, yl, z, core


def enter(devices):
    barrier = pltpu.get_barrier_semaphore()
    for device in devices:
        pl.semaphore_signal(barrier, inc=1, device_id=device, device_id_type=MESH)
    pl.semaphore_wait(barrier, len(devices))


def unpack(words, scale, j):
    levels = (words & (7 << (3 * j))).astype(F32).astype(BF16) - jnp.asarray(4.0 * 8.0**j, BF16)
    return levels * (scale * 8.0**-j).astype(BF16)


CH = 13


def gate_up_kernel(
    tok, gcodes, ucodes, gs, us, flip, out,
    gbuf, ubuf, w, xg, pb, r1, r2, s3, r3, own,
    ld, ys, yr, ps, pr, ss, sr, cs, cr, r1s, r1r, r2s, r2r, r3s, r3r,
):
    dp, t, x, yh, yl, z, core = place()
    yo = 1 - yl
    sign = 1 - 2 * core
    tid = lambda a, b, c: a * 16 + b * 2 + c
    zat = lambda k: lax.rem(z + sign * k + 8, 8)
    dev_y = (dp, tid(yo, z, core))
    dev_c = (dp, tid(yl, z, 1 - core))
    dev_p = (dp, tid(yl, zat(1), core))
    dev_s = (dp, tid(yl, zat(-1), core))
    xr, xl, x2 = lax.rem(x + 1, 4), lax.rem(x + 3, 4), lax.rem(x + 2, 4)
    dev_r = (xr * 2 + yh, t)
    dev_l = (xl * 2 + yh, t)
    dev_h = (x * 2 + 1 - yh, t)

    loads = [pltpu.make_async_copy(gcodes, gbuf, ld.at[0]), pltpu.make_async_copy(ucodes, ubuf, ld.at[1])]
    for copy in loads:
        copy.start()

    rows_i = lax.broadcasted_iota(jnp.int32, (512, 512), 0)
    cols_i = lax.broadcasted_iota(jnp.int32, (512, 512), 1)
    pick = jnp.where(rows_i == 4 * (cols_i % 128) + cols_i // 128, 1.0, 0.0).astype(BF16)
    for q in range(4):
        cols = slice(512 * q, 512 * q + 512)
        xg[yl, z, core, :, cols] = jnp.dot(tok[:, cols], pick, preferred_element_type=F32).astype(BF16)

    enter([dev_y, dev_c, dev_p, dev_s, dev_r, dev_l, dev_h])

    yv = (yl, yo)

    def copy_y(y):
        return remote(xg.at[y, z, core], xg.at[y, z, core], ys.at[0], yr.at[0], dev_y)

    def copy_p(k, yy, away):
        block = xg.at[yv[yy], zat(-away), core]
        return remote(block, block, ps.at[k - 1, yy], pr.at[k - 1, yy], dev_p)

    def copy_s(k, yy, away):
        block = xg.at[yv[yy], zat(away), core]
        return remote(block, block, ss.at[k - 1, yy], sr.at[k - 1, yy], dev_s)

    def copy_c(slot, yy, back, c):
        block = xg.at[yv[yy], zat(back), c]
        return remote(block, block, cs.at[slot, yy], cr.at[slot, yy], dev_c)

    def dequant(c, carry):
        cols = pl.ds(pl.multiple_of(128 * c, 128), 128)
        for side, (buf, sc) in enumerate(((gbuf, gs), (ubuf, us))):
            for g in range(16):
                words = buf[32 * g : 32 * g + 32, cols]
                scale = sc[g : g + 1, cols]
                for j in range(4):
                    row = 512 * (g // 4) + 128 * j + 32 * (g % 4)
                    w[c, row : row + 32, 128 * side : 128 * side + 128] = unpack(words, scale, j)
        return carry

    sends = []

    def go(copy):
        copy.start()
        sends.append(copy)

    go(copy_y(yl))
    go(copy_p(1, 0, 0))
    go(copy_s(1, 0, 0))
    go(copy_c(0, 0, 0, core))
    for copy in loads:
        copy.wait()
    lax.fori_loop(0, 1, dequant, 0)
    copy_y(yo).wait_recv()
    go(copy_p(1, 1, 0))
    go(copy_s(1, 1, 0))
    go(copy_c(0, 1, 0, core))
    spans = {1: (1, 4), 2: (4, 7), 3: (7, 10), 4: (10, 13)}
    for k in range(1, 5):
        for yy in range(2):
            copy_p(k, yy, k).wait_recv()
            if k < 4:
                go(copy_p(k + 1, yy, k))
            go(copy_c(k, yy, -k, core))
            if k < 4:
                copy_s(k, yy, k).wait_recv()
                if k < 3:
                    go(copy_s(k + 1, yy, k))
                go(copy_c(4 + k, yy, k, core))
        lax.fori_loop(*spans[k], dequant, 0)
    for slot in range(8):
        back = slot if slot < 5 else -(slot - 4)
        for yy in range(2):
            copy_c(slot, yy, back, 1 - core).wait_recv()

    def first(c):
        far_a = pb.at[c, pl.ds(pl.multiple_of(128 * x2, 64), 64)]
        far_b = pb.at[c, pl.ds(pl.multiple_of(128 * x2 + 64, 64), 64)]
        return (
            remote(far_a, r1.at[0, c], r1s.at[0, c], r1r.at[0, c], dev_r),
            remote(far_b, r1.at[1, c], r1s.at[1, c], r1r.at[1, c], dev_l),
        )

    def second(c):
        near_r = pb.at[c, pl.ds(pl.multiple_of(128 * xr, 128), 128)]
        near_l = pb.at[c, pl.ds(pl.multiple_of(128 * xl, 128), 128)]
        return (
            remote(near_r, r2.at[0, c], r2s.at[0, c], r2r.at[0, c], dev_r),
            remote(near_l, r2.at[1, c], r2s.at[1, c], r2r.at[1, c], dev_l),
        )

    def third(c):
        return remote(s3.at[c], r3.at[c], r3s.at[c], r3r.at[c], dev_h)

    def multiply(c, carry):
        both = jnp.dot(xg[...].reshape(512, 2048), w[c], preferred_element_type=F32)
        pb[c] = both.astype(BF16)
        for copy in first(c):
            copy.start()
        return carry

    def round_two(c, carry):
        arrive, leave = first(c), second(c)
        arrive[0].wait_recv()
        rows = pl.ds(pl.multiple_of(128 * xr, 64), 64)
        pb[c, rows] = (pb[c, rows].astype(F32) + r1[0, c].astype(F32)).astype(BF16)
        leave[0].start()
        arrive[1].wait_recv()
        rows = pl.ds(pl.multiple_of(128 * xl + 64, 64), 64)
        pb[c, rows] = (pb[c, rows].astype(F32) + r1[1, c].astype(F32)).astype(BF16)
        leave[1].start()
        return carry

    def round_three(c, carry):
        arrive = second(c)
        arrive[0].wait_recv()
        arrive[1].wait_recv()

        def total(half):
            here = pl.ds(pl.multiple_of(128 * x + 64 * half, 64), 64)
            there = pl.ds(pl.multiple_of(64 * half, 64), 64)
            return pb[c, here].astype(F32) + r2[0, c, there].astype(F32) + r2[1, c, there].astype(F32)

        s3[c] = total(1 - yh).astype(BF16)
        third(c).start()
        own[c] = total(yh)
        return carry

    def finish(c, carry):
        third(c).wait_recv()
        full = own[c] + r3[c].astype(F32)
        gate, up = full[:, :128], full[:, 128:]
        cols = pl.ds(pl.multiple_of(128 * c, 128), 128)
        hidden = (gate / (1.0 + jnp.exp(-gate)) * up).astype(BF16).astype(F32)
        out[:, cols] = jnp.where(flip[:, cols] == 1, hidden, -hidden).astype(BF16)
        return carry

    def drain(c, carry):
        for copy in first(c) + second(c) + (third(c),):
            copy.wait_send()
        return carry

    for step in (multiply, round_two, round_three, finish, drain):
        lax.fori_loop(0, CH, step, 0)
    for copy in sends:
        copy.wait_send()


def gate_up(tokens, gate_codes, gate_scales, up_codes, up_scales, flip_signs):
    vm = pl.BlockSpec(memory_space=pltpu.VMEM)
    hbm = pl.BlockSpec(memory_space=pl.ANY)
    dma = pltpu.SemaphoreType.DMA
    return pl.pallas_call(
        gate_up_kernel,
        out_shape=jax.ShapeDtypeStruct((64, 1664), BF16),
        in_specs=[vm, hbm, hbm, vm, vm, vm],
        out_specs=vm,
        scratch_shapes=[
            pltpu.VMEM((512, 1664), jnp.int32),
            pltpu.VMEM((512, 1664), jnp.int32),
            pltpu.VMEM((CH, 2048, 256), BF16),
            pltpu.VMEM((2, 8, 2, 16, 2048), BF16),
            pltpu.VMEM((CH, 512, 256), BF16),
            pltpu.VMEM((2, CH, 64, 256), BF16),
            pltpu.VMEM((2, CH, 128, 256), BF16),
            pltpu.VMEM((CH, 64, 256), BF16),
            pltpu.VMEM((CH, 64, 256), BF16),
            pltpu.VMEM((CH, 64, 256), F32),
            dma((2,)), dma((1,)), dma((1,)),
            dma((4, 2)), dma((4, 2)), dma((3, 2)), dma((3, 2)), dma((8, 2)), dma((8, 2)),
            dma((2, CH)), dma((2, CH)), dma((2, CH)), dma((2, CH)), dma((CH,)), dma((CH,)),
        ],
        compiler_params=pltpu.CompilerParams(
            collective_id=0, has_side_effects=True, vmem_limit_bytes=VMEM_LIMIT
        ),
        cost_estimate=pl.CostEstimate(flops=7 * 10**9, bytes_accessed=10**7, transcendentals=10**5),
    )(tokens, gate_codes, up_codes, gate_scales.astype(F32), up_scales.astype(F32), flip_signs[None, :])


HAND = 26


def rotate_kernel(hid, table_hbm, out, table, gin, gout, hm, ld, as_, ar, bs, br):
    dp, t, x, yh, yl, z, core = place()
    load = pltpu.make_async_copy(table_hbm, table, ld.at[0])
    load.start()
    others = [lax.rem(t + k, 32) for k in range(1, 32)]
    enter([(dp, o) for o in others])

    def tile(ref, o):
        return ref.at[pl.ds(pl.multiple_of(32 * lax.rem(o, 2), 32), 32), pl.ds(pl.multiple_of(128 * lax.div(o, 2), 128), 128)]

    def ahead(o):
        return remote(tile(hid, o), gin.at[t], as_.at[o], ar.at[t], (dp, o))

    def back(o):
        return remote(gout.at[o], tile(hm, t), bs.at[o], br.at[t], (dp, o))

    def send_ahead(k, carry):
        o = lax.rem(t + k, 32)

        @pl.when(o < HAND)
        def _():
            ahead(o).start()

        return carry

    lax.fori_loop(1, 32, send_ahead, 0)

    @pl.when(t < HAND)
    def _():
        gin[t] = tile(hid, t)[...]

        def arrive(k, carry):
            o = lax.rem(t + k, 32)
            remote(gin.at[o], gin.at[o], as_.at[o], ar.at[o], (dp, o)).wait_recv()
            return carry

        lax.fori_loop(1, 32, arrive, 0)
        for half in range(2):
            rows = slice(16 * half, 16 * half + 16)
            values = [gin[g, rows].astype(F32) for g in range(32)]
            for bit in range(5):
                step = 1 << bit
                values = [
                    values[g] + values[g + step] if g & step == 0 else values[g - step] - values[g]
                    for g in range(32)
                ]
            for g in range(32):
                gout[g, rows] = values[g].astype(BF16)

        def send_back(k, carry):
            back(lax.rem(t + k, 32)).start()
            return carry

        lax.fori_loop(1, 32, send_back, 0)
        tile(hm, t)[...] = gout[t]

    def arrive_back(k, carry):
        o = lax.rem(t + k, 32)

        @pl.when(o < HAND)
        def _():
            remote(gout.at[o], tile(hm, o), bs.at[o], br.at[o], (dp, o)).wait_recv()

        return carry

    lax.fori_loop(1, 32, arrive_back, 0)
    load.wait()
    out[...] = (jnp.dot(hm[...], table[...], preferred_element_type=F32) * FF**-0.5).astype(BF16)

    def drain(k, carry):
        o = lax.rem(t + k, 32)

        @pl.when(o < HAND)
        def _():
            ahead(o).wait_send()

        @pl.when(t < HAND)
        def _():
            back(o).wait_send()

        return carry

    lax.fori_loop(1, 32, drain, 0)


def rotate(hidden):
    vm = pl.BlockSpec(memory_space=pltpu.VMEM)
    hbm = pl.BlockSpec(memory_space=pl.ANY)
    dma = pltpu.SemaphoreType.DMA
    return pl.pallas_call(
        rotate_kernel,
        out_shape=jax.ShapeDtypeStruct((64, 1664), BF16),
        in_specs=[vm, hbm],
        out_specs=vm,
        scratch_shapes=[
            pltpu.VMEM((1664, 1664), BF16),
            pltpu.VMEM((32, 32, 128), BF16),
            pltpu.VMEM((32, 32, 128), BF16),
            pltpu.VMEM((64, 1664), BF16),
            dma((1,)), dma((32,)), dma((32,)), dma((32,)), dma((32,)),
        ],
        compiler_params=pltpu.CompilerParams(
            collective_id=1, has_side_effects=True, vmem_limit_bytes=VMEM_LIMIT
        ),
        cost_estimate=pl.CostEstimate(flops=4 * 10**8, bytes_accessed=6 * 10**6, transcendentals=0),
    )(hidden, jnp.asarray(inner_table(), dtype=BF16))


NC = 4
WC = 512


def down_kernel(
    rot, dcodes, ds_, out,
    dbuf, w, rg, pb, rc, rz1, rz, tot, ry,
    ld, ags, agr, ccs, ccr, zs, zr, yys, yyr,
):
    dp, t, x, yh, yl, z, core = place()
    ho, yo = 1 - yh, 1 - yl
    xr, xl, x2 = lax.rem(x + 1, 4), lax.rem(x + 3, 4), lax.rem(x + 2, 4)
    tid = lambda a, b, c: a * 16 + b * 2 + c
    zat = lambda k: lax.rem(z + k + 8, 8)
    dev_r, dev_l, dev_h = (xr * 2 + yh, t), (xl * 2 + yh, t), (x * 2 + ho, t)
    dev_y, dev_c = (dp, tid(yo, z, core)), (dp, tid(yl, z, 1 - core))
    dev_u, dev_d = (dp, tid(yl, zat(1), core)), (dp, tid(yl, zat(-1), core))

    load = pltpu.make_async_copy(dcodes, dbuf, ld.at[0])
    load.start()
    rg[dp] = rot[...]
    enter([dev_r, dev_l, dev_h, dev_y, dev_c, dev_u, dev_d])

    def block(kind, dev, slot):
        b = rg.at[kind]
        return remote(b, b, ags.at[slot], agr.at[slot], dev)

    mine, mate = x * 2 + yh, x * 2 + ho
    sends = [block(mine, dev_h, 0), block(mine, dev_r, 1), block(mine, dev_l, 2)]
    for copy in sends:
        copy.start()

    load.wait()

    def dequant(c, carry):
        cols = pl.ds(pl.multiple_of(128 * c, 128), 128)
        for g in range(13):
            words = dbuf[32 * g : 32 * g + 32, cols]
            scale = ds_[g : g + 1, cols]
            for j in range(4):
                row = 416 * j + 32 * g
                w[row : row + 32, cols] = unpack(words, scale, j)
        return carry

    lax.fori_loop(0, 4, dequant, 0)
    block(mate, dev_h, 0).wait_recv()
    more = [block(mate, dev_r, 3), block(mate, dev_l, 4)]
    for copy in more:
        copy.start()
    block(xl * 2 + yh, dev_r, 1).wait_recv()
    more.append(block(xl * 2 + yh, dev_r, 5))
    more[-1].start()
    lax.fori_loop(4, 10, dequant, 0)
    block(xr * 2 + ho, dev_l, 4).wait_recv()
    more.append(block(xr * 2 + ho, dev_l, 6))
    more[-1].start()
    lax.fori_loop(10, 16, dequant, 0)
    block(xr * 2 + yh, dev_l, 2).wait_recv()
    block(xl * 2 + ho, dev_r, 3).wait_recv()
    block(x2 * 2 + yh, dev_r, 5).wait_recv()
    block(x2 * 2 + ho, dev_l, 6).wait_recv()

    def pair(c):
        return remote(pb.at[c, 1 - core], rc.at[c], ccs.at[c], ccr.at[c], dev_c)

    def one(c):
        return (
            remote(pb.at[c, core, 0, zat(4)], rz1.at[0, c], zs.at[0, 0, c], zr.at[0, 0, c], dev_u),
            remote(pb.at[c, core, 1, zat(4)], rz1.at[1, c], zs.at[1, 0, c], zr.at[1, 0, c], dev_d),
        )

    def ring(r, c):
        k = 5 - r
        return (
            remote(pb.at[c, core, :, zat(k)], rz.at[0, r - 2, c], zs.at[0, r - 1, c], zr.at[0, r - 1, c], dev_u),
            remote(pb.at[c, core, :, zat(-k)], rz.at[1, r - 2, c], zs.at[1, r - 1, c], zr.at[1, r - 1, c], dev_d),
        )

    def across(c):
        return remote(tot.at[c, yo], ry.at[c], yys.at[c], yyr.at[c], dev_y)

    def multiply(c, carry):
        for part in range(2):
            cols = pl.ds(pl.multiple_of(WC * c + 256 * part, 256), 256)
            terms = jnp.dot(rg[...].reshape(512, 1664), w[:, cols], preferred_element_type=F32).astype(BF16)
            for cc in range(2):
                for yy in range(2):
                    for zz in range(8):
                        row = 16 * (16 * yy + 2 * zz + cc)
                        pb[c, cc, yy, zz, :, 256 * part : 256 * part + 256] = terms[row : row + 16]
        pair(c).start()
        return carry

    def round_one(c, carry):
        pair(c).wait_recv()
        pb[c, core] = (pb[c, core].astype(F32) + rc[c].astype(F32)).astype(BF16)
        for copy in one(c):
            copy.start()
        return carry

    def round_two(c, carry):
        for side in range(2):
            one(c)[side].wait_recv()
            at = zat(3 - 6 * side)
            pb[c, core, side, at] = (pb[c, core, side, at].astype(F32) + rz1[side, c].astype(F32)).astype(BF16)
            ring(2, c)[side].start()
        return carry

    def round_more(r, c, carry):
        for side in range(2):
            ring(r - 1, c)[side].wait_recv()
            at = zat((5 - r) * (1 - 2 * side))
            for yy in range(2):
                pb[c, core, yy, at] = (
                    pb[c, core, yy, at].astype(F32) + rz[side, r - 3, c, yy].astype(F32)
                ).astype(BF16)
            ring(r, c)[side].start()
        return carry

    def round_last(c, carry):
        for side in range(2):
            ring(4, c)[side].wait_recv()
        for yy in range(2):
            tot[c, yy] = (
                pb[c, core, yy, z].astype(F32) + rz[0, 2, c, yy].astype(F32) + rz[1, 2, c, yy].astype(F32)
            ).astype(BF16)
        across(c).start()
        return carry

    def finish(c, carry):
        across(c).wait_recv()
        cols = pl.ds(pl.multiple_of(WC * c, WC), WC)
        out[:, cols] = (tot[c, yl].astype(F32) + ry[c].astype(F32)).astype(BF16)
        return carry

    def drain(c, carry):
        for copy in (pair(c),) + one(c) + ring(2, c) + ring(3, c) + ring(4, c) + (across(c),):
            copy.wait_send()
        return carry

    steps = (
        multiply, round_one, round_two,
        functools.partial(round_more, 3), functools.partial(round_more, 4),
        round_last, finish, drain,
    )
    for step in steps:
        lax.fori_loop(0, NC, step, 0)
    for copy in sends + more:
        copy.wait_send()


def down(rotated, down_codes, down_scales):
    vm = pl.BlockSpec(memory_space=pltpu.VMEM)
    hbm = pl.BlockSpec(memory_space=pl.ANY)
    dma = pltpu.SemaphoreType.DMA
    return pl.pallas_call(
        down_kernel,
        out_shape=jax.ShapeDtypeStruct((16, 2048), BF16),
        in_specs=[vm, hbm, vm],
        out_specs=vm,
        scratch_shapes=[
            pltpu.VMEM((416, 2048), jnp.int32),
            pltpu.VMEM((1664, 2048), BF16),
            pltpu.VMEM((8, 64, 1664), BF16),
            pltpu.VMEM((NC, 2, 2, 8, 16, WC), BF16),
            pltpu.VMEM((NC, 2, 8, 16, WC), BF16),
            pltpu.VMEM((2, NC, 16, WC), BF16),
            pltpu.VMEM((2, 3, NC, 2, 16, WC), BF16),
            pltpu.VMEM((NC, 2, 16, WC), BF16),
            pltpu.VMEM((NC, 16, WC), BF16),
            dma((1,)), dma((7,)), dma((7,)), dma((NC,)), dma((NC,)),
            dma((2, 4, NC)), dma((2, 4, NC)), dma((NC,)), dma((NC,)),
        ],
        compiler_params=pltpu.CompilerParams(
            collective_id=2, has_side_effects=True, vmem_limit_bytes=VMEM_LIMIT
        ),
        cost_estimate=pl.CostEstimate(flops=4 * 10**9, bytes_accessed=4 * 10**6, transcendentals=0),
    )(rotated, down_codes, down_scales.astype(F32))


def per_device(
    tokens, gate_codes, gate_scales, up_codes, up_scales, down_codes, down_scales, flip_signs
):
    hidden = gate_up(tokens, gate_codes, gate_scales, up_codes, up_scales, flip_signs)
    return down(rotate(hidden), down_codes, down_scales)


def solution(mesh):
    return jax.shard_map(
        per_device,
        mesh=mesh,
        in_specs=(
            P("tensor", "dp"),
            P("dp", "tensor"),
            P("dp", "tensor"),
            P("dp", "tensor"),
            P("dp", "tensor"),
            P("tensor", "dp"),
            P("tensor", "dp"),
            P("tensor"),
        ),
        out_specs=P("tensor", "dp"),
        check_vma=False,
    )
```

```python
import functools

import jax
import jax.numpy as jnp
import numpy as np
from jax import lax
from jax.experimental import pallas as pl
from jax.experimental.pallas import tpu as pltpu
from jax.sharding import PartitionSpec as P

FF = 53248
KB = 52
BLK = 32
MESH = pl.DeviceIdType.MESH
BF16 = jnp.bfloat16
F32 = jnp.float32
VMEM_LIMIT = 60 * 1024 * 1024


def paley_table():
    field_square = np.zeros(25, dtype=np.int64)
    for first_part in range(5):
        for second_part in range(5):
            if first_part == 0 and second_part == 0:
                continue
            real_part = (first_part * first_part + 2 * second_part * second_part) % 5
            root_part = 2 * first_part * second_part % 5
            field_square[real_part + 5 * root_part] = 1
    character = np.where(field_square == 1, 1, -1)
    character[0] = 0
    jacobsthal = np.zeros((25, 25), dtype=np.int64)
    for left_item in range(25):
        for right_item in range(25):
            diff_real = (left_item % 5 - right_item % 5) % 5
            diff_root = (left_item // 5 - right_item // 5) % 5
            jacobsthal[left_item, right_item] = character[diff_real + 5 * diff_root]
    conference = np.zeros((26, 26), dtype=np.int64)
    conference[0, 1:] = 1
    conference[1:, 0] = 1
    conference[1:, 1:] = jacobsthal
    outer_part = np.array([[1, -1], [-1, -1]], dtype=np.int64)
    inner_part = np.array([[1, 1], [1, -1]], dtype=np.int64)
    return np.kron(conference, outer_part) + np.kron(np.eye(26, dtype=np.int64), inner_part)


def sylvester_static(order_size):
    position = np.arange(order_size)
    parity = np.zeros((order_size, order_size), dtype=np.int64)
    for bit_place in range(max(order_size.bit_length() - 1, 0)):
        parity = parity + (position[:, None] >> bit_place & position[None, :] >> bit_place & 1)
    return 1 - 2 * (parity & 1)


def inner_table():
    table = np.kron(paley_table(), sylvester_static(BLK))
    order = (4 * np.arange(416)[None, :] + np.arange(4)[:, None]).reshape(-1)
    return table[:, order].astype(np.float32)


def remote(src, dst, send_sem, recv_sem, device):
    return pltpu.make_async_remote_copy(
        src_ref=src, dst_ref=dst, send_sem=send_sem, recv_sem=recv_sem, device_id=device, device_id_type=MESH
    )


def place():
    dp = lax.axis_index("dp")
    t = lax.axis_index("tensor")
    x, yh = lax.div(dp, 2), lax.rem(dp, 2)
    yl, z, core = lax.div(t, 16), lax.rem(lax.div(t, 2), 8), lax.rem(t, 2)
    return dp, t, x, yh, yl, z, core


def unpack(words, scale, j):
    levels = (words & (7 << (3 * j))).astype(F32).astype(BF16) - jnp.asarray(4.0 * 8.0**j, BF16)
    return levels * (scale * 8.0**-j).astype(BF16)


CH = 13
GROUPS = ((0, 4, True, True), (4, 3, True, True), (7, 3, True, True), (10, 3, False, False))
ORDER = (0, 1, 3, 2)
NC = 4
WC = 512


def kernel(
    tok, gcodes, ucodes, dcodes, gs, us, ds_, flip, table_hbm, out,
    cbuf, ubuf, w, xg, pb, r1, r2, ry, s3, r3, own,
    table, hid, gin, gout, rg, acc, wd, rot,
    qb, rc, rz1, rz, tot, rl,
    ld, ys, yr, ps, pr, ss, sr, cs, cr, as_, ar, bs, br, r1s, r1r, r2s, r2r, r3s, r3r, ags, agr,
    ccs, ccr, zs, zr, yys, yyr,
):
    dp, t, x, yh, yl, z, core = place()
    ho, yo, co = 1 - yh, 1 - yl, 1 - core
    sign = 1 - 2 * core
    tid = lambda a, b, c: a * 16 + b * 2 + c
    zat = lambda k: lax.rem(z + k + 8, 8)
    zsg = lambda k: lax.rem(z + sign * k + 8, 8)
    xr, xl, x2 = lax.rem(x + 1, 4), lax.rem(x + 3, 4), lax.rem(x + 2, 4)
    dev_y, dev_c = (dp, tid(yo, z, core)), (dp, tid(yl, z, co))
    dev_p, dev_s = (dp, tid(yl, zsg(1), core)), (dp, tid(yl, zsg(-1), core))
    dev_u, dev_d = (dp, tid(yl, zat(1), core)), (dp, tid(yl, zat(-1), core))
    dev_r, dev_l, dev_h = (xr * 2 + yh, t), (xl * 2 + yh, t), (x * 2 + ho, t)

    gbuf, dbuf = cbuf.at[:, pl.ds(0, 1664)], cbuf.at[pl.ds(0, 416)]
    load_g = pltpu.make_async_copy(gcodes, gbuf, ld.at[0])
    load_u = pltpu.make_async_copy(ucodes, ubuf, ld.at[1])
    load_t = pltpu.make_async_copy(table_hbm, table, ld.at[2])
    load_d = pltpu.make_async_copy(dcodes, dbuf, ld.at[3])
    load_g.start()
    load_u.start()

    rows_i = lax.broadcasted_iota(jnp.int32, (512, 512), 0)
    cols_i = lax.broadcasted_iota(jnp.int32, (512, 512), 1)
    pick = jnp.where(rows_i == 4 * (cols_i % 128) + cols_i // 128, 1.0, 0.0).astype(BF16)
    for q in range(4):
        cols = slice(512 * q, 512 * q + 512)
        xg[yl, z, core, :, cols] = jnp.dot(tok[:, cols], pick, preferred_element_type=F32).astype(BF16)

    barrier = pltpu.get_barrier_semaphore()
    for device in (dev_r, dev_l, dev_h):
        pl.semaphore_signal(barrier, inc=1, device_id=device, device_id_type=MESH)

    def greet(k, carry):
        pl.semaphore_signal(barrier, inc=1, device_id=(dp, lax.rem(t + k, 32)), device_id_type=MESH)
        return carry

    lax.fori_loop(1, 32, greet, 0)
    pl.semaphore_wait(barrier, 34)

    sends = []

    def go(copy):
        copy.start()
        sends.append(copy)

    yv = (yl, yo)

    def piece(y, back, c, h):
        return xg.at[y, zsg(back), c, :, pl.ds(1024 * h, 1024)]

    def copy_y(y, back, slot, h):
        block = piece(y, back, core, h)
        return remote(block, block, ys.at[slot, h], yr.at[slot, h], dev_y)

    def copy_p(k, yy, away, h):
        block = piece(yv[yy], -away, core, h)
        return remote(block, block, ps.at[k - 1, yy, h], pr.at[k - 1, yy, h], dev_p)

    def copy_s(k, yy, away, h):
        block = piece(yv[yy], away, core, h)
        return remote(block, block, ss.at[k - 1, yy, h], sr.at[k - 1, yy, h], dev_s)

    def copy_c(slot, yy, back, c, h):
        block = piece(yv[yy], back, c, h)
        return remote(block, block, cs.at[slot, yy, h], cr.at[slot, yy, h], dev_c)

    def dequant(c, carry):
        cols = pl.ds(pl.multiple_of(128 * c, 128), 128)
        for side, (buf, sc) in enumerate(((gbuf, gs), (ubuf, us))):
            scales = sc[:, cols].astype(F32)
            for g in range(16):
                words = buf[32 * g : 32 * g + 32, cols]
                for j in range(4):
                    row = 512 * (g // 4) + 128 * j + 32 * (g % 4)
                    w[c, row : row + 32, 128 * side : 128 * side + 128] = unpack(words, scales[g : g + 1], j)
        return carry

    def forward(k, yy, last_p, last_s):
        for h in range(2):
            copy_p(k, yy, k, h).wait_recv()
            if k < last_p:
                go(copy_p(k + 1, yy, k, h))
            if yy == 0 and k >= 3:
                go(copy_y(yl, -k, k - 2, h))
            go(copy_c(k, yy, -k, core, h))
            if k <= last_s:
                copy_s(k, yy, k, h).wait_recv()
                if k < last_s:
                    go(copy_s(k + 1, yy, k, h))
                if yy == 0 and k >= 3:
                    go(copy_y(yl, k, 3, h))
                go(copy_c(4 + k, yy, k, core, h))

    for h in range(2):
        go(copy_p(1, 0, 0, h))
        go(copy_s(1, 0, 0, h))
        go(copy_y(yl, 0, 0, h))
    for h in range(2):
        go(copy_c(0, 0, 0, core, h))
    load_g.wait()
    load_u.wait()
    lax.fori_loop(0, 3, dequant, 0)
    forward(1, 0, 4, 3)
    for h in range(2):
        copy_y(yo, 0, 0, h).wait_recv()
        go(copy_p(1, 1, 0, h))
        go(copy_s(1, 1, 0, h))
        go(copy_c(0, 1, 0, core, h))
    lax.fori_loop(3, 6, dequant, 0)
    forward(2, 0, 4, 3)
    lax.fori_loop(6, 8, dequant, 0)
    forward(1, 1, 2, 2)
    lax.fori_loop(8, 10, dequant, 0)
    forward(3, 0, 4, 3)
    lax.fori_loop(10, 13, dequant, 0)
    load_t.start()
    load_d.start()
    forward(2, 1, 2, 2)
    forward(4, 0, 4, 3)
    for back, way, slot in ((-3, 1, 3), (3, 3, 7), (-4, 2, 4)):
        for h in range(2):
            copy_y(yo, back, way, h).wait_recv()
            go(copy_c(slot, 1, back, core, h))
    for yy in range(2):
        for slot in range(8):
            for h in range(2):
                copy_c(slot, yy, slot if slot < 5 else 4 - slot, co, h).wait_recv()

    def x_far(c, x_first):
        if x_first:
            a, b = pb.at[c, x2, 0], pb.at[c, x2, 1]
            to_a, to_b = r1.at[c, 0], r1.at[c, 1]
        else:
            a, b = pb.at[c, x2, yh, pl.ds(0, 32)], pb.at[c, x2, yh, pl.ds(32, 32)]
            to_a, to_b = r1.at[c, 0, pl.ds(0, 32)], r1.at[c, 1, pl.ds(0, 32)]
        return (
            remote(a, to_a, r1s.at[c, 0], r1r.at[c, 0], dev_r),
            remote(b, to_b, r1s.at[c, 1], r1r.at[c, 1], dev_l),
        )

    def x_near(c, x_first):
        if x_first:
            a, b, to_a, to_b = pb.at[c, xr], pb.at[c, xl], r2.at[c, 0], r2.at[c, 1]
        else:
            a, b, to_a, to_b = pb.at[c, xr, yh], pb.at[c, xl, yh], r2.at[c, 0, 0], r2.at[c, 1, 0]
        return (
            remote(a, to_a, r2s.at[c, 0], r2r.at[c, 0], dev_r),
            remote(b, to_b, r2s.at[c, 1], r2r.at[c, 1], dev_l),
        )

    def y_swap(c, x_first):
        if x_first:
            return remote(s3.at[c], r3.at[c], r3s.at[c], r3r.at[c], dev_h)
        return remote(pb.at[c, :, ho], ry.at[c], r3s.at[c], r3r.at[c], dev_h)

    def add_far(c, x_first):
        arrive, leave = x_far(c, x_first), x_near(c, x_first)
        for side, at in ((0, xr), (1, xl)):
            arrive[side].wait_recv()
            if x_first:
                pb[c, at, side] = (pb[c, at, side].astype(F32) + r1[c, side].astype(F32)).astype(BF16)
            else:
                rows = pl.ds(32 * side, 32)
                pb[c, at, yh, rows] = (
                    pb[c, at, yh, rows].astype(F32) + r1[c, side, 0:32].astype(F32)
                ).astype(BF16)
            leave[side].start()

    def multiply(x_first, c, carry):
        both = jnp.dot(xg[...].reshape(512, 2048), w[c], preferred_element_type=F32)
        pb[c] = both.astype(BF16).reshape(4, 2, 64, 256)
        for copy in x_far(c, True) if x_first else (y_swap(c, False),):
            copy.start()
        return carry

    def stage_two(x_first, c, carry):
        if x_first:
            add_far(c, True)
        else:
            y_swap(c, False).wait_recv()
            for at in range(4):
                pb[c, at, yh] = (pb[c, at, yh].astype(F32) + ry[c, at].astype(F32)).astype(BF16)
            for copy in x_far(c, False):
                copy.start()
        return carry

    def stage_three(x_first, c, carry):
        if x_first:
            arrive = x_near(c, True)
            arrive[0].wait_recv()
            arrive[1].wait_recv()

            def total(half):
                return pb[c, x, half].astype(F32) + r2[c, 0, half].astype(F32) + r2[c, 1, half].astype(F32)

            s3[c] = total(ho).astype(BF16)
            y_swap(c, True).start()
            own[c] = total(yh)
        else:
            add_far(c, False)
        return carry

    def owner(i):
        u = lax.rem(i, 32)
        return 2 * lax.rem(u, 16) + lax.div(u, 16)

    def a2a_out(i):
        slot = lax.div(i, 32)
        return remote(hid.at[i], gin.at[slot, t], as_.at[i], ar.at[slot, t], (dp, owner(i)))

    def stage_four(x_first, c, carry):
        if x_first:
            y_swap(c, True).wait_recv()
            full = own[c] + r3[c].astype(F32)
        else:
            arrive = x_near(c, False)
            arrive[0].wait_recv()
            arrive[1].wait_recv()
            full = pb[c, x, yh].astype(F32) + r2[c, 0, 0].astype(F32) + r2[c, 1, 0].astype(F32)
        gate, up = full[:, :128], full[:, 128:]
        signs = flip[pl.ds(pl.multiple_of(128 * c, 128), 128)].reshape(1, 128)
        hidden = (gate / (1.0 + jnp.exp(-gate)) * up).astype(BF16).astype(F32)
        flipped = jnp.where(signs == 1, hidden, -hidden).astype(BF16)
        for h in range(4):
            hid[4 * c + h] = flipped[16 * h : 16 * h + 16]

            @pl.when(owner(4 * c + h) != t)
            def _():
                a2a_out(4 * c + h).start()

        return carry

    mine = 16 * core + lax.div(t, 2)

    def tile(i):
        rows = pl.ds(pl.multiple_of(16 * lax.rem(i, 4), 16), 16)
        return rg.at[dp, rows, pl.ds(pl.multiple_of(128 * lax.div(i, 4), 128), 128)]

    def a2a_back(slot, o):
        i = mine + 32 * slot
        return remote(gout.at[slot, o], tile(i), bs.at[slot, o], br.at[i], (dp, o))

    def handle(first, count):
        for slot in range(2):
            i = mine + 32 * slot
            if 32 * slot >= 4 * (first + count) or 32 * slot + 32 <= 4 * first:
                continue

            @pl.when((i >= 4 * first) & (i < 4 * (first + count)))
            def _():
                gin[slot, t] = hid[i]

                def arrive(k, carry):
                    o = lax.rem(t + k, 32)
                    remote(gin.at[slot, o], gin.at[slot, o], as_.at[0], ar.at[slot, o], (dp, o)).wait_recv()
                    return carry

                lax.fori_loop(1, 32, arrive, 0)
                values = [gin[slot, g].astype(F32) for g in range(32)]
                for bit in range(5):
                    step = 1 << bit
                    values = [
                        values[g] + values[g + step] if g & step == 0 else values[g - step] - values[g]
                        for g in range(32)
                    ]
                for g in range(32):
                    gout[slot, g] = values[g].astype(BF16)

                def send(k, carry):
                    a2a_back(slot, lax.rem(t + k, 32)).start()
                    return carry

                lax.fori_loop(1, 32, send, 0)
                tile(i)[...] = gout[slot, t]

    def spread(g, slot, at, half, device, rows=slice(0, 64)):
        first, count = GROUPS[g][:2]
        block = rg.at[2 * at + half, pl.ds(rows.start, rows.stop - rows.start), pl.ds(128 * first, 128 * count)]
        return remote(block, block, ags.at[g, slot], agr.at[g, slot], device)

    top, low = slice(0, 32), slice(32, 64)

    def gather_one(g):
        first, count = GROUPS[g][:2]

        def arrive(i, carry):
            @pl.when(owner(i) != t)
            def _():
                remote(gout.at[0, 0], tile(i), bs.at[0, 0], br.at[i], (dp, owner(i))).wait_recv()

            return carry

        lax.fori_loop(4 * first, 4 * (first + count), arrive, 0)
        for slot, device in enumerate((dev_r, dev_l, dev_h)):
            go(spread(g, slot, x, yh, device))

    def gather_two(g):
        if GROUPS[g][3]:
            spread(g, 0, xl, yh, dev_r).wait_recv()
            go(spread(g, 3, xl, yh, dev_r, top))
            go(spread(g, 5, xl, yh, dev_h))
            spread(g, 1, xr, yh, dev_l).wait_recv()
            go(spread(g, 4, xr, yh, dev_l, low))
            go(spread(g, 6, xr, yh, dev_h))
        else:
            spread(g, 0, xl, yh, dev_r).wait_recv()
            go(spread(g, 5, xl, yh, dev_r))
            spread(g, 2, x, ho, dev_h).wait_recv()
            go(spread(g, 3, x, ho, dev_r))
            go(spread(g, 4, x, ho, dev_l))

    def gather_three(g):
        if GROUPS[g][3]:
            spread(g, 3, x2, yh, dev_r, top).wait_recv()
            spread(g, 4, x2, yh, dev_l, low).wait_recv()
            go(spread(g, 7, x2, yh, dev_h))
        else:
            spread(g, 4, xr, ho, dev_l).wait_recv()
            go(spread(g, 6, xr, ho, dev_l))

    def gather_wait(g):
        if GROUPS[g][3]:
            spread(g, 2, x, ho, dev_h).wait_recv()
            spread(g, 5, xl, ho, dev_h).wait_recv()
            spread(g, 6, xr, ho, dev_h).wait_recv()
            spread(g, 7, x2, ho, dev_h).wait_recv()
        else:
            spread(g, 1, xr, yh, dev_l).wait_recv()
            spread(g, 3, xl, ho, dev_r).wait_recv()
            spread(g, 5, x2, yh, dev_r).wait_recv()
            spread(g, 6, x2, ho, dev_l).wait_recv()

    def inner(g):
        gather_wait(g)
        first, count = GROUPS[g][:2]
        rows = slice(128 * first, 128 * (first + count))

        def columns(cols):
            part = jnp.dot(
                rg[:, :, rows].reshape(512, 128 * count), table[rows, cols], preferred_element_type=F32
            )
            if g != ORDER[0]:
                part = part + acc[:, cols]
            if g != ORDER[-1]:
                acc[:, cols] = part
            else:
                rot[:, cols] = (part * FF**-0.5).astype(BF16)

        def step(n, carry):
            columns(pl.ds(pl.multiple_of(256 * n, 256), 256))
            return carry

        lax.fori_loop(0, 6, step, 0)
        columns(pl.ds(1536, 128))

    def dequant_down(c, carry):
        cols = pl.ds(pl.multiple_of(128 * c, 128), 128)
        scales = ds_[:, cols].astype(F32)
        for g in range(13):
            words = dbuf[32 * g : 32 * g + 32, cols]
            for j in range(4):
                row = 416 * j + 32 * g
                wd[row : row + 32, cols] = unpack(words, scales[g : g + 1], j)
        return carry

    def run(stage, g):
        first, count, x_first = GROUPS[g][:3]
        lax.fori_loop(first, first + count, functools.partial(stage, x_first), 0)

    def H(g):
        handle(GROUPS[g][0], GROUPS[g][1])

    M, S2, S3, S4 = (functools.partial(run, stage) for stage in (multiply, stage_two, stage_three, stage_four))
    T1, T2, T3, I = gather_one, gather_two, gather_three, inner

    def unpack_down():
        load_t.wait()
        load_d.wait()
        lax.fori_loop(0, 16, dequant_down, 0)

    M(0), M(3), M(1), S2(0), M(2), S2(1)
    unpack_down()
    S3(0), S2(3), S2(2), S4(0), S3(1), S3(3), H(0), S4(1), S3(2), T1(0), H(1), S4(3), T2(0), H(3), T1(1), S4(2), T3(0)
    H(2), T1(3), T2(1), I(0), T2(3), T3(1), T1(2), T3(3), T2(2), I(1), T3(2), I(3), I(2)

    def pair(c):
        return remote(qb.at[c, co], rc.at[c], ccs.at[c], ccr.at[c], dev_c)

    def one(c):
        return (
            remote(qb.at[c, core, 0, zat(4)], rz1.at[0, c], zs.at[0, 0, c], zr.at[0, 0, c], dev_u),
            remote(qb.at[c, core, 1, zat(4)], rz1.at[1, c], zs.at[1, 0, c], zr.at[1, 0, c], dev_d),
        )

    def ring(r, c):
        k = 5 - r
        return (
            remote(qb.at[c, core, :, zat(k)], rz.at[0, r - 2, c], zs.at[0, r - 1, c], zr.at[0, r - 1, c], dev_u),
            remote(qb.at[c, core, :, zat(-k)], rz.at[1, r - 2, c], zs.at[1, r - 1, c], zr.at[1, r - 1, c], dev_d),
        )

    def across(c):
        return remote(tot.at[c, yo], rl.at[c], yys.at[c], yyr.at[c], dev_y)

    def down(c, carry):
        for part in range(2):
            cols = pl.ds(pl.multiple_of(WC * c + 256 * part, 256), 256)
            terms = jnp.dot(rot[...], wd[:, cols], preferred_element_type=F32).astype(BF16)
            for cc in range(2):
                for yy in range(2):
                    for zz in range(8):
                        row = 16 * (16 * yy + 2 * zz + cc)
                        qb[c, cc, yy, zz, :, 256 * part : 256 * part + 256] = terms[row : row + 16]
        pair(c).start()
        return carry

    def round_one(c, carry):
        pair(c).wait_recv()
        qb[c, core] = (qb[c, core].astype(F32) + rc[c].astype(F32)).astype(BF16)
        for copy in one(c):
            copy.start()
        return carry

    def round_two(c, carry):
        for side in range(2):
            one(c)[side].wait_recv()
            at = zat(3 - 6 * side)
            qb[c, core, side, at] = (qb[c, core, side, at].astype(F32) + rz1[side, c].astype(F32)).astype(BF16)
            ring(2, c)[side].start()
        return carry

    def round_more(r, c, carry):
        for side in range(2):
            ring(r - 1, c)[side].wait_recv()
            at = zat((5 - r) * (1 - 2 * side))
            for yy in range(2):
                qb[c, core, yy, at] = (
                    qb[c, core, yy, at].astype(F32) + rz[side, r - 3, c, yy].astype(F32)
                ).astype(BF16)
            ring(r, c)[side].start()
        return carry

    def round_last(c, carry):
        for side in range(2):
            ring(4, c)[side].wait_recv()
        for yy in range(2):
            tot[c, yy] = (
                qb[c, core, yy, z].astype(F32) + rz[0, 2, c, yy].astype(F32) + rz[1, 2, c, yy].astype(F32)
            ).astype(BF16)
        across(c).start()
        return carry

    def finish(c, carry):
        across(c).wait_recv()
        cols = pl.ds(pl.multiple_of(WC * c, WC), WC)
        out[:, cols] = (tot[c, yl].astype(F32) + rl[c].astype(F32)).astype(BF16)
        return carry

    def start(c, carry):
        down(c, carry)

        @pl.when(c >= 1)
        def _():
            round_one(c - 1, carry)

        @pl.when(c >= 2)
        def _():
            round_two(c - 2, carry)

        return carry

    lax.fori_loop(0, NC, start, 0)
    round_one(NC - 1, 0)
    round_two(NC - 2, 0)
    round_two(NC - 1, 0)
    steps = (functools.partial(round_more, 3), functools.partial(round_more, 4), round_last, finish)
    for step in steps:
        lax.fori_loop(0, NC, step, 0)

    def drain_down(c, carry):
        for copy in (pair(c),) + one(c) + ring(2, c) + ring(3, c) + ring(4, c) + (across(c),):
            copy.wait_send()
        return carry

    def drain_up(x_first, c, carry):
        for copy in x_far(c, x_first) + x_near(c, x_first) + (y_swap(c, x_first),):
            copy.wait_send()
        for h in range(4):

            @pl.when(owner(4 * c + h) != t)
            def _():
                a2a_out(4 * c + h).wait_send()

        return carry

    lax.fori_loop(0, NC, drain_down, 0)
    for g in range(len(GROUPS)):
        run(drain_up, g)

    for slot in range(2):

        @pl.when(mine + 32 * slot < 4 * CH)
        def _():
            def drain_back(k, carry):
                a2a_back(slot, lax.rem(t + k, 32)).wait_send()
                return carry

            lax.fori_loop(1, 32, drain_back, 0)

    for copy in sends:
        copy.wait_send()


def per_device(
    tokens, gate_codes, gate_scales, up_codes, up_scales, down_codes, down_scales, flip_signs
):
    vm = pl.BlockSpec(memory_space=pltpu.VMEM)
    hbm = pl.BlockSpec(memory_space=pl.ANY)
    dma = pltpu.SemaphoreType.DMA
    ng = len(GROUPS)
    return pl.pallas_call(
        kernel,
        out_shape=jax.ShapeDtypeStruct((16, 2048), BF16),
        in_specs=[vm, hbm, hbm, hbm, vm, vm, vm, vm, hbm],
        out_specs=vm,
        scratch_shapes=[
            pltpu.VMEM((512, 2048), jnp.int32),
            pltpu.VMEM((512, 1664), jnp.int32),
            pltpu.VMEM((CH, 2048, 256), BF16),
            pltpu.VMEM((2, 8, 2, 16, 2048), BF16),
            pltpu.VMEM((CH, 4, 2, 64, 256), BF16),
            pltpu.VMEM((CH, 2, 64, 256), BF16),
            pltpu.VMEM((CH, 2, 2, 64, 256), BF16),
            pltpu.VMEM((CH, 4, 64, 256), BF16),
            pltpu.VMEM((CH, 64, 256), BF16),
            pltpu.VMEM((CH, 64, 256), BF16),
            pltpu.VMEM((CH, 64, 256), F32),
            pltpu.VMEM((1664, 1664), BF16),
            pltpu.VMEM((4 * CH, 16, 128), BF16),
            pltpu.VMEM((2, 32, 16, 128), BF16),
            pltpu.VMEM((2, 32, 16, 128), BF16),
            pltpu.VMEM((8, 64, 1664), BF16),
            pltpu.VMEM((512, 1664), F32),
            pltpu.VMEM((1664, 2048), BF16),
            pltpu.VMEM((512, 1664), BF16),
            pltpu.VMEM((NC, 2, 2, 8, 16, WC), BF16),
            pltpu.VMEM((NC, 2, 8, 16, WC), BF16),
            pltpu.VMEM((2, NC, 16, WC), BF16),
            pltpu.VMEM((2, 3, NC, 2, 16, WC), BF16),
            pltpu.VMEM((NC, 2, 16, WC), BF16),
            pltpu.VMEM((NC, 16, WC), BF16),
            dma((4,)), dma((4, 2)), dma((4, 2)),
            dma((4, 2, 2)), dma((4, 2, 2)), dma((3, 2, 2)), dma((3, 2, 2)), dma((8, 2, 2)), dma((8, 2, 2)),
            dma((4 * CH,)), dma((2, 32)), dma((2, 32)), dma((4 * CH,)),
            dma((CH, 2)), dma((CH, 2)), dma((CH, 2)), dma((CH, 2)), dma((CH,)), dma((CH,)),
            dma((ng, 8)), dma((ng, 8)),
            dma((NC,)), dma((NC,)), dma((2, 4, NC)), dma((2, 4, NC)), dma((NC,)), dma((NC,)),
        ],
        compiler_params=pltpu.CompilerParams(
            collective_id=0, has_side_effects=True, vmem_limit_bytes=VMEM_LIMIT
        ),
        cost_estimate=pl.CostEstimate(flops=14 * 10**9, bytes_accessed=2 * 10**7, transcendentals=10**5),
    )(
        tokens, gate_codes, up_codes, down_codes, gate_scales, up_scales, down_scales,
        flip_signs, jnp.asarray(inner_table(), dtype=BF16),
    )


def solution(mesh):
    return jax.shard_map(
        per_device,
        mesh=mesh,
        in_specs=(
            P("tensor", "dp"),
            P("dp", "tensor"),
            P("dp", "tensor"),
            P("dp", "tensor"),
            P("dp", "tensor"),
            P("tensor", "dp"),
            P("tensor", "dp"),
            P("tensor"),
        ),
        out_specs=P("tensor", "dp"),
        check_vma=False,
    )
```

```python
import functools

import jax
import jax.numpy as jnp
import numpy as np
from jax import lax
from jax.experimental import pallas as pl
from jax.experimental.pallas import tpu as pltpu
from jax.sharding import PartitionSpec as P

FF = 53248
KB = 52
BLK = 32
MESH = pl.DeviceIdType.MESH
BF16 = jnp.bfloat16
F32 = jnp.float32
VMEM_LIMIT = 60 * 1024 * 1024


def paley_table():
    field_square = np.zeros(25, dtype=np.int64)
    for first_part in range(5):
        for second_part in range(5):
            if first_part == 0 and second_part == 0:
                continue
            real_part = (first_part * first_part + 2 * second_part * second_part) % 5
            root_part = 2 * first_part * second_part % 5
            field_square[real_part + 5 * root_part] = 1
    character = np.where(field_square == 1, 1, -1)
    character[0] = 0
    jacobsthal = np.zeros((25, 25), dtype=np.int64)
    for left_item in range(25):
        for right_item in range(25):
            diff_real = (left_item % 5 - right_item % 5) % 5
            diff_root = (left_item // 5 - right_item // 5) % 5
            jacobsthal[left_item, right_item] = character[diff_real + 5 * diff_root]
    conference = np.zeros((26, 26), dtype=np.int64)
    conference[0, 1:] = 1
    conference[1:, 0] = 1
    conference[1:, 1:] = jacobsthal
    outer_part = np.array([[1, -1], [-1, -1]], dtype=np.int64)
    inner_part = np.array([[1, 1], [1, -1]], dtype=np.int64)
    return np.kron(conference, outer_part) + np.kron(np.eye(26, dtype=np.int64), inner_part)


def sylvester_static(order_size):
    position = np.arange(order_size)
    parity = np.zeros((order_size, order_size), dtype=np.int64)
    for bit_place in range(max(order_size.bit_length() - 1, 0)):
        parity = parity + (position[:, None] >> bit_place & position[None, :] >> bit_place & 1)
    return 1 - 2 * (parity & 1)


def inner_table():
    table = np.kron(paley_table(), sylvester_static(BLK))
    order = (4 * np.arange(416)[None, :] + np.arange(4)[:, None]).reshape(-1)
    return table[:, order].astype(np.float32)


def remote(src, dst, send_sem, recv_sem, device):
    return pltpu.make_async_remote_copy(
        src_ref=src, dst_ref=dst, send_sem=send_sem, recv_sem=recv_sem, device_id=device, device_id_type=MESH
    )


def place():
    dp = lax.axis_index("dp")
    t = lax.axis_index("tensor")
    x, yh = lax.div(dp, 2), lax.rem(dp, 2)
    yl, z, core = lax.div(t, 16), lax.rem(lax.div(t, 2), 8), lax.rem(t, 2)
    return dp, t, x, yh, yl, z, core


def unpack(words, scale, j):
    levels = (words & (7 << (3 * j))).astype(F32).astype(BF16) - jnp.asarray(4.0 * 8.0**j, BF16)
    return levels * (scale * 8.0**-j).astype(BF16)


CH = 13
GROUPS = ((0, 3, False, "2"), (3, 3, True, "y"), (6, 3, False, "y"), (9, 4, True, "x"))
ORDER = (1, 0, 2, 3)
NC = 4
WC = 512


def kernel(
    tok, gcodes, ucodes, dcodes, gs, us, ds_, flip, table_hbm, out,
    cbuf, ubuf, w, xg, pb, r1, r2, ry, s3, r3, own,
    table, hid, gin, gout, rg, acc, wd,
    qb, rc, rz1, rz, rl,
    ld, sd, as_, bs, ar, br, cr, yr, pr, sr, r1r, r2r, r3r, agr, ccr, zr, yyr,
):
    dp, t, x, yh, yl, z, core = place()
    ho, yo, co = 1 - yh, 1 - yl, 1 - core
    sign = 1 - 2 * core
    tid = lambda a, b, c: a * 16 + b * 2 + c
    zat = lambda k: lax.rem(z + k + 8, 8)
    zsg = lambda k: lax.rem(z + sign * k + 8, 8)
    xr, xl, x2 = lax.rem(x + 1, 4), lax.rem(x + 3, 4), lax.rem(x + 2, 4)
    dev_y, dev_c = (dp, tid(yo, z, core)), (dp, tid(yl, z, co))
    dev_p, dev_s = (dp, tid(yl, zsg(1), core)), (dp, tid(yl, zsg(-1), core))
    dev_u, dev_d = (dp, tid(yl, zat(1), core)), (dp, tid(yl, zat(-1), core))
    dev_r, dev_l, dev_h = (xr * 2 + yh, t), (xl * 2 + yh, t), (x * 2 + ho, t)

    barrier = pltpu.get_barrier_semaphore()
    for device in (dev_r, dev_l, dev_h):
        pl.semaphore_signal(barrier, inc=1, device_id=device, device_id_type=MESH)

    def greet(k, carry):
        pl.semaphore_signal(barrier, inc=1, device_id=(dp, lax.rem(t + k, 32)), device_id_type=MESH)
        return carry

    lax.fori_loop(1, 32, greet, 0)
    gbuf, dbuf = cbuf.at[:, pl.ds(0, 1664)], cbuf.at[pl.ds(0, 416)]
    load_g = pltpu.make_async_copy(gcodes, gbuf, ld.at[0])
    load_u = pltpu.make_async_copy(ucodes, ubuf, ld.at[1])
    load_t = pltpu.make_async_copy(table_hbm, table, ld.at[2])
    load_d = pltpu.make_async_copy(dcodes, dbuf, ld.at[3])
    load_g.start()
    load_u.start()

    rows_i = lax.broadcasted_iota(jnp.int32, (512, 512), 0)
    cols_i = lax.broadcasted_iota(jnp.int32, (512, 512), 1)
    pick = jnp.where(rows_i == 4 * (cols_i % 128) + cols_i // 128, 1.0, 0.0).astype(BF16)
    for q in range(4):
        cols = slice(512 * q, 512 * q + 512)
        xg[yl, z, core, :, cols] = jnp.dot(tok[:, cols], pick, preferred_element_type=F32).astype(BF16)

    pl.semaphore_wait(barrier, 34)

    sent = [0, 0, 0, 0]

    def size(ref):
        return int(np.prod(ref.shape)) * 2

    def push(phase, src, dst, recv_sem, device, times=1):
        sent[phase] += size(src) * times
        return remote(src, dst, sd.at[phase], recv_sem, device)

    def settle(phase):
        rows = sent[phase] // 512
        for outer in range(1, CH + 1):
            if rows % outer == 0 and rows // outer % 16 == 0 and rows // outer <= 2048:
                span = w.at[pl.ds(0, outer), pl.ds(0, rows // outer)]
                pltpu.make_async_copy(span, span, sd.at[phase]).wait()
                return
        raise ValueError(rows)

    def landed(ref, sem):
        pltpu.make_async_copy(ref, ref, sem).wait()

    yv = (yl, yo)

    def piece(y, back, c, h):
        return xg.at[y, zsg(back), c, :, pl.ds(1024 * h, 1024)]

    def copy_y(y, back, slot, h):
        block = piece(y, back, core, h)
        return block, yr.at[slot, h], dev_y

    def copy_p(k, yy, away, h):
        block = piece(yv[yy], -away, core, h)
        return block, pr.at[k - 1, yy, h], dev_p

    def copy_s(k, yy, away, h):
        block = piece(yv[yy], away, core, h)
        return block, sr.at[k - 1, yy, h], dev_s

    def copy_c(slot, yy, back, h):
        return piece(yv[yy], back, core, h), cr.at[0], dev_c

    def go(copy):
        block, sem, device = copy
        push(0, block, block, sem, device).start()

    def come(copy):
        landed(copy[0], copy[1])

    def dequant(c, carry):
        cols = pl.ds(pl.multiple_of(128 * c, 128), 128)
        for side, (buf, sc) in enumerate(((gbuf, gs), (ubuf, us))):
            scales = sc[:, cols].astype(F32)
            for g in range(16):
                words = buf[32 * g : 32 * g + 32, cols]
                for j in range(4):
                    row = 512 * (g // 4) + 128 * j + 32 * (g % 4)
                    w[c, row : row + 32, 128 * side : 128 * side + 128] = unpack(words, scales[g : g + 1], j)
        return carry

    def ring(k, yy, h, reach_p=4, reach_s=3):
        if k <= reach_p:
            come(copy_p(k, yy, k, h))
            if k < 4:
                go(copy_p(k + 1, yy, k, h))
            if h == 0:
                go(copy_y(yl, -k, k, h))
            go(copy_c(k, yy, -k, h))
        if k <= reach_s:
            come(copy_s(k, yy, k, h))
            if k < 3:
                go(copy_s(k + 1, yy, k, h))
            if h == 0:
                go(copy_y(yl, k, 4 + k, h))
            go(copy_c(4 + k, yy, k, h))

    go(copy_y(yl, 0, 0, 1))
    for h in range(2):
        go(copy_p(1, 0, 0, h))
        go(copy_s(1, 0, 0, h))
    go(copy_y(yl, 0, 0, 0))
    for h in range(2):
        go(copy_c(0, 0, 0, h))
    load_g.wait()
    load_u.wait()
    lax.fori_loop(0, 2, dequant, 0)
    ring(1, 0, 0)
    come(copy_y(yo, 0, 0, 1))
    go(copy_p(1, 1, 0, 1))
    go(copy_s(1, 1, 0, 1))
    ring(1, 0, 1)
    come(copy_y(yo, 0, 0, 0))
    for h in range(2):
        go(copy_c(0, 1, 0, h))
    lax.fori_loop(2, 4, dequant, 0)
    ring(2, 0, 0)
    ring(1, 1, 1)
    ring(2, 0, 1)
    lax.fori_loop(4, 6, dequant, 0)
    ring(3, 0, 0)
    ring(2, 1, 1)
    ring(3, 0, 1)
    lax.fori_loop(6, 9, dequant, 0)
    ring(4, 0, 0)
    ring(3, 1, 1)
    ring(4, 0, 1)
    lax.fori_loop(9, 13, dequant, 0)
    load_t.start()
    load_d.start()
    for back, way, slot in ((-1, 1, 1), (1, 5, 5), (-2, 2, 2), (2, 6, 6), (-3, 3, 3), (3, 7, 7), (-4, 4, 4)):
        come(copy_y(yo, back, way, 0))
        go(copy_c(slot, 1, back, 0))
    ring(4, 1, 1)
    landed(w.at[0], cr.at[0])

    def x_far(c, x_first, times):
        if x_first:
            a, b = pb.at[c, x2, 0], pb.at[c, x2, 1]
            to_a, to_b = r1.at[c, 0], r1.at[c, 1]
        else:
            a, b = pb.at[c, x2, yh, pl.ds(0, 32)], pb.at[c, x2, yh, pl.ds(32, 32)]
            to_a, to_b = r1.at[c, 0, pl.ds(0, 32)], r1.at[c, 1, pl.ds(0, 32)]
        push(1, a, to_a, r1r.at[c], dev_r, times).start()
        push(1, b, to_b, r1r.at[c], dev_l, times).start()

    def x_near(c, x_first, times):
        if x_first:
            a, b, to_a, to_b = pb.at[c, xr], pb.at[c, xl], r2.at[c, 0], r2.at[c, 1]
        else:
            a, b, to_a, to_b = pb.at[c, xr, yh], pb.at[c, xl, yh], r2.at[c, 0, 0], r2.at[c, 1, 0]
        push(1, a, to_a, r2r.at[c], dev_r, times).start()
        push(1, b, to_b, r2r.at[c], dev_l, times).start()

    def add_far(c, x_first, times):
        landed(r1.at[c] if x_first else r1.at[c, 0], r1r.at[c])
        for side, at in ((0, xr), (1, xl)):
            if x_first:
                pb[c, at, side] = (pb[c, at, side].astype(F32) + r1[c, side].astype(F32)).astype(BF16)
            else:
                rows = pl.ds(32 * side, 32)
                pb[c, at, yh, rows] = (
                    pb[c, at, yh, rows].astype(F32) + r1[c, side, 0:32].astype(F32)
                ).astype(BF16)
        x_near(c, x_first, times)

    def multiply(x_first, times, c, carry):
        both = jnp.dot(xg[...].reshape(512, 2048), w[c], preferred_element_type=F32)
        pb[c] = both.astype(BF16).reshape(4, 2, 64, 256)
        if x_first:
            x_far(c, True, times)
        else:
            push(1, pb.at[c, :, ho], ry.at[c], r3r.at[c], dev_h, times).start()
        return carry

    def stage_two(x_first, times, c, carry):
        if x_first:
            add_far(c, True, times)
        else:
            landed(ry.at[c], r3r.at[c])
            for at in range(4):
                pb[c, at, yh] = (pb[c, at, yh].astype(F32) + ry[c, at].astype(F32)).astype(BF16)
            x_far(c, False, times)
        return carry

    def stage_three(x_first, times, c, carry):
        if x_first:
            landed(r2.at[c], r2r.at[c])

            def total(half):
                return pb[c, x, half].astype(F32) + r2[c, 0, half].astype(F32) + r2[c, 1, half].astype(F32)

            s3[c] = total(ho).astype(BF16)
            push(1, s3.at[c], r3.at[c], r3r.at[c], dev_h, times).start()
            own[c] = total(yh)
        else:
            add_far(c, False, times)
        return carry

    def owner(i):
        u = lax.rem(i, 32)
        return 2 * lax.rem(u, 16) + lax.div(u, 16)

    def a2a_out(i):
        slot = lax.div(i, 32)
        return remote(hid.at[i], gin.at[slot, t], as_.at[0], ar.at[slot], (dp, owner(i)))

    def stage_four(x_first, times, c, carry):
        if x_first:
            landed(r3.at[c], r3r.at[c])
            full = own[c] + r3[c].astype(F32)
        else:
            landed(r2.at[c, 0], r2r.at[c])
            full = pb[c, x, yh].astype(F32) + r2[c, 0, 0].astype(F32) + r2[c, 1, 0].astype(F32)
        gate, up = full[:, :128], full[:, 128:]
        signs = flip[pl.ds(pl.multiple_of(128 * c, 128), 128)].reshape(1, 128)
        hidden = (gate / (1.0 + jnp.exp(-gate)) * up).astype(BF16).astype(F32)
        flipped = jnp.where(signs == 1, hidden, -hidden).astype(BF16)
        for h in range(4):
            hid[4 * c + h] = flipped[16 * h : 16 * h + 16]

            @pl.when(owner(4 * c + h) != t)
            def _():
                a2a_out(4 * c + h).start()

        return carry

    mine = 16 * core + lax.div(t, 2)

    def tile(i):
        rows = pl.ds(pl.multiple_of(16 * lax.rem(i, 4), 16), 16)
        return rg.at[dp, rows, pl.ds(pl.multiple_of(128 * lax.div(i, 4), 128), 128)]

    def group_of(i):
        found = 0
        for first, _, _, _ in GROUPS[1:]:
            found = found + jnp.where(i >= 4 * first, 1, 0)
        return found

    def a2a_back(slot, o):
        i = mine + 32 * slot
        return remote(gout.at[slot, o], tile(i), bs.at[slot], br.at[group_of(i)], (dp, o))

    def handle(first, count):
        for slot in range(2):
            i = mine + 32 * slot
            if 32 * slot >= 4 * (first + count) or 32 * slot + 32 <= 4 * first:
                continue

            @pl.when((i >= 4 * first) & (i < 4 * (first + count)))
            def _():
                gin[slot, t] = hid[i]

                landed(gin.at[slot, pl.ds(0, 31)], ar.at[slot])
                values = [gin[slot, g].astype(F32) for g in range(32)]
                for bit in range(5):
                    step = 1 << bit
                    values = [
                        values[g] + values[g + step] if g & step == 0 else values[g - step] - values[g]
                        for g in range(32)
                    ]
                for g in range(32):
                    gout[slot, g] = values[g].astype(BF16)

                def send(k, carry):
                    a2a_back(slot, lax.rem(t + k, 32)).start()
                    return carry

                lax.fori_loop(1, 32, send, 0)
                tile(i)[...] = gout[slot, t]

    def block(g, at, half, rows=slice(0, 64)):
        first, count = GROUPS[g][:2]
        return rg.at[2 * at + half, pl.ds(rows.start, rows.stop - rows.start), pl.ds(128 * first, 128 * count)]

    def blocks(g, n):
        first, count = GROUPS[g][:2]
        return rg.at[pl.ds(0, n), :, pl.ds(128 * first, 128 * count)]

    def spread(g, sem, at, half, device, rows=slice(0, 64)):
        part = block(g, at, half, rows)
        push(2, part, part, agr.at[g, sem], device).start()

    top, low = slice(0, 32), slice(32, 64)

    def gather_one(g):
        first, count, _, kind = GROUPS[g]
        inside = False
        for slot in range(2):
            i = mine + 32 * slot
            inside = inside | ((i >= 4 * first) & (i < 4 * (first + count)))

        @pl.when(inside)
        def _():
            landed(hid.at[pl.ds(0, 4 * count - 1)], br.at[g])

        @pl.when(jnp.logical_not(inside))
        def _():
            landed(hid.at[pl.ds(0, 4 * count)], br.at[g])

        if kind == "x":
            spread(g, 0, x, yh, dev_r)
            spread(g, 1, x, yh, dev_l)
            spread(g, 3, x, yh, dev_h)
        elif kind == "2":
            for sem, device in enumerate((dev_r, dev_l, (x2 * 2 + yh, t), dev_h)):
                spread(g, sem, x, yh, device)
        elif kind == "y":
            spread(g, 0, x, yh, dev_h)
            spread(g, 1, x, yh, dev_r)
            spread(g, 3, x, yh, dev_l)
        else:
            for half in (ho, yh):
                for to in (x2, xr, xl, x):
                    if half is ho or to is not x:
                        spread(g, 3, x, yh, (to * 2 + half, t))

    def gather_two(g):
        if GROUPS[g][3] == "x":
            landed(block(g, xl, yh), agr.at[g, 0])
            spread(g, 2, xl, yh, dev_r, top)
            spread(g, 3, xl, yh, dev_h)
            landed(block(g, xr, yh), agr.at[g, 1])
            spread(g, 2, xr, yh, dev_l, low)
            spread(g, 3, xr, yh, dev_h)
        elif GROUPS[g][3] == "2":
            for sem, at in enumerate((xl, xr, x2)):
                landed(block(g, at, yh), agr.at[g, sem])
                spread(g, 3, at, yh, dev_h)
        else:
            landed(block(g, xl, yh), agr.at[g, 1])
            spread(g, 3, xl, yh, dev_r)
            landed(block(g, x, ho), agr.at[g, 0])
            spread(g, 3, x, ho, dev_r)
            spread(g, 2, x, ho, dev_l)

    def gather_three(g):
        if GROUPS[g][3] == "x":
            landed(block(g, x2, yh), agr.at[g, 2])
            spread(g, 3, x2, yh, dev_h)
        else:
            landed(block(g, xr, ho), agr.at[g, 2])
            spread(g, 3, xr, ho, dev_l)

    def gather_wait(g):
        landed(blocks(g, 7 if GROUPS[g][3] == "d" else 4), agr.at[g, 3])

    def fold(n):
        cols = pl.ds(256 * n, 256)
        for part in range(2):
            rows = pl.ds(832 * part, 832)
            product = jnp.dot(table[rows, :], wd[:, cols], preferred_element_type=F32)
            w[n, rows] = (product * FF**-0.5).astype(BF16)

    def terms_of(g, n):
        first, count = GROUPS[g][:2]
        rows = pl.ds(128 * first, 128 * count)
        units = rg[:, :, 128 * first : 128 * (first + count)].reshape(512, 128 * count)
        return jnp.dot(units, w[n, rows], preferred_element_type=F32)

    def accumulate(g):
        gather_wait(g)

        def step(n, carry):
            cols = pl.ds(pl.multiple_of(256 * n, 256), 256)
            terms = terms_of(g, n)
            acc[:, cols] = terms if g == ORDER[0] else acc[:, cols] + terms
            return carry

        lax.fori_loop(0, 8, step, 0)

    def dequant_down(c, carry):
        cols = pl.ds(pl.multiple_of(128 * c, 128), 128)
        scales = ds_[:, cols].astype(F32)
        for g in range(13):
            words = dbuf[32 * g : 32 * g + 32, cols]
            for j in range(4):
                row = 416 * j + 32 * g
                wd[row : row + 32, cols] = unpack(words, scales[g : g + 1], j)
        return carry

    def run(stage, g):
        first, count, x_first = GROUPS[g][:3]
        lax.fori_loop(first, first + count, functools.partial(stage, x_first, count), 0)

    def H(g):
        handle(GROUPS[g][0], GROUPS[g][1])

    M, S2, S3, S4 = (functools.partial(run, stage) for stage in (multiply, stage_two, stage_three, stage_four))
    T1, T2, T3, W, A = gather_one, gather_two, gather_three, fold, accumulate

    def unpack_down():
        load_t.wait()
        load_d.wait()
        lax.fori_loop(0, 16, dequant_down, 0)

    M(0), M(1), M(3), S2(1), M(2), S2(0), S2(3)
    unpack_down()
    W(0), S3(1), S3(0), W(1), W(2), S2(2), S3(3), W(3), S4(1), S4(0), S3(2), S4(3), S4(2), H(1), H(0), H(3), H(2)
    T1(1), T1(0), W(4), T2(1), T1(2), T1(3), W(5), T2(0), W(6), T3(1), T2(2), W(7), T2(3), A(1), T3(2), T3(3), A(0), A(2)

    def pair(c):
        push(3, qb.at[c, co], rc.at[c], ccr.at[c], dev_c, NC).start()

    def z_one(c, times):
        push(3, qb.at[c, core, 0, zat(4)], rz1.at[c, 0], zr.at[0, c], dev_u, times).start()
        push(3, qb.at[c, core, 1, zat(4)], rz1.at[c, 1], zr.at[0, c], dev_d, times).start()
        push(3, qb.at[c, core, yo, z], rl.at[c], yyr.at[c], dev_y, times).start()

    def down(c):
        for part in range(2):
            n = 2 * c + part
            cols = pl.ds(pl.multiple_of(256 * n, 256), 256)
            terms = (acc[:, cols] + terms_of(ORDER[-1], n)).astype(BF16)
            for cc in range(2):
                for yy in range(2):
                    for zz in range(8):
                        row = 16 * (16 * yy + 2 * zz + cc)
                        qb[c, cc, yy, zz, :, 256 * part : 256 * part + 256] = terms[row : row + 16]
        pair(c)

    def after_pair(times, c):
        landed(rc.at[c], ccr.at[c])
        qb[c, core] = (qb[c, core].astype(F32) + rc[c].astype(F32)).astype(BF16)
        z_one(c, times)

    def z_round(r, c, carry):
        landed(rz1.at[c] if r == 2 else rz.at[r - 3, c], zr.at[r - 2, c])
        for side in range(2):
            at = zat((5 - r) * (1 - 2 * side))
            if r == 2:
                qb[c, core, side, at] = (qb[c, core, side, at].astype(F32) + rz1[c, side].astype(F32)).astype(BF16)
            else:
                for yy in range(2):
                    qb[c, core, yy, at] = (
                        qb[c, core, yy, at].astype(F32) + rz[r - 3, c, side, yy].astype(F32)
                    ).astype(BF16)
            if r < 4:
                push(3, qb.at[c, core, :, at], rz.at[r - 2, c, side], zr.at[r - 1, c], (dev_u, dev_d)[side], NC).start()
            else:
                for row, to in ((0, yl), (1, yo)):
                    device = (dp, tid(to, at, core))
                    push(3, qb.at[c, core, to, at], rz.at[2, c, side, row], zr.at[3, c], device, NC).start()
        return carry

    def finish(c, carry):
        landed(rl.at[c], yyr.at[c])
        landed(rz.at[2, c], zr.at[3, c])
        total = qb[c, core, yl, z].astype(F32) + rl[c].astype(F32)
        for side in range(2):
            for row in range(2):
                total = total + rz[2, c, side, row].astype(F32)
        cols = pl.ds(pl.multiple_of(WC * c, WC), WC)
        out[:, cols] = total.astype(BF16)
        return carry

    gather_wait(ORDER[-1])

    def start(c, carry):
        down(c)

        @pl.when(c > 0)
        def _():
            after_pair(NC - 1, c - 1)

        return carry

    lax.fori_loop(0, NC, start, 0)
    after_pair(1, NC - 1)
    for step in (functools.partial(z_round, 2), functools.partial(z_round, 3), functools.partial(z_round, 4), finish):
        lax.fori_loop(0, NC, step, 0)

    for phase in range(4):
        settle(phase)
    for slot in range(2):
        i = mine + 32 * slot

        @pl.when(i < 4 * CH)
        def _():
            landed(gout.at[slot, pl.ds(0, 31)], bs.at[slot])

    two = mine + 32 < 4 * CH

    @pl.when(two)
    def _():
        landed(hid.at[pl.ds(0, 4 * CH - 2)], as_.at[0])

    @pl.when(jnp.logical_not(two))
    def _():
        landed(hid.at[pl.ds(0, 4 * CH - 1)], as_.at[0])


def per_device(
    tokens, gate_codes, gate_scales, up_codes, up_scales, down_codes, down_scales, flip_signs
):
    vm = pl.BlockSpec(memory_space=pltpu.VMEM)
    hbm = pl.BlockSpec(memory_space=pl.ANY)
    dma = pltpu.SemaphoreType.DMA
    ng = len(GROUPS)
    return pl.pallas_call(
        kernel,
        out_shape=jax.ShapeDtypeStruct((16, 2048), BF16),
        in_specs=[vm, hbm, hbm, hbm, vm, vm, vm, vm, hbm],
        out_specs=vm,
        scratch_shapes=[
            pltpu.VMEM((512, 2048), jnp.int32),
            pltpu.VMEM((512, 1664), jnp.int32),
            pltpu.VMEM((CH, 2048, 256), BF16),
            pltpu.VMEM((2, 8, 2, 16, 2048), BF16),
            pltpu.VMEM((CH, 4, 2, 64, 256), BF16),
            pltpu.VMEM((CH, 2, 64, 256), BF16),
            pltpu.VMEM((CH, 2, 2, 64, 256), BF16),
            pltpu.VMEM((CH, 4, 64, 256), BF16),
            pltpu.VMEM((CH, 64, 256), BF16),
            pltpu.VMEM((CH, 64, 256), BF16),
            pltpu.VMEM((CH, 64, 256), F32),
            pltpu.VMEM((1664, 1664), BF16),
            pltpu.VMEM((4 * CH, 16, 128), BF16),
            pltpu.VMEM((2, 32, 16, 128), BF16),
            pltpu.VMEM((2, 32, 16, 128), BF16),
            pltpu.VMEM((8, 64, 1664), BF16),
            pltpu.VMEM((512, 2048), F32),
            pltpu.VMEM((1664, 2048), BF16),
            pltpu.VMEM((NC, 2, 2, 8, 16, WC), BF16),
            pltpu.VMEM((NC, 2, 8, 16, WC), BF16),
            pltpu.VMEM((NC, 2, 16, WC), BF16),
            pltpu.VMEM((3, NC, 2, 2, 16, WC), BF16),
            pltpu.VMEM((NC, 16, WC), BF16),
            dma((4,)), dma((4,)), dma((1,)), dma((2,)), dma((2,)), dma((ng,)), dma((1,)),
            dma((8, 2)), dma((4, 2, 2)), dma((3, 2, 2)), dma((CH,)), dma((CH,)), dma((CH,)), dma((ng, 4)),
            dma((NC,)), dma((4, NC)), dma((NC,)),
        ],
        compiler_params=pltpu.CompilerParams(
            collective_id=0, has_side_effects=True, vmem_limit_bytes=VMEM_LIMIT
        ),
        cost_estimate=pl.CostEstimate(flops=14 * 10**9, bytes_accessed=2 * 10**7, transcendentals=10**5),
    )(
        tokens, gate_codes, up_codes, down_codes, gate_scales, up_scales, down_scales,
        flip_signs, jnp.asarray(inner_table(), dtype=BF16),
    )


def solution(mesh):
    return jax.shard_map(
        per_device,
        mesh=mesh,
        in_specs=(
            P("tensor", "dp"),
            P("dp", "tensor"),
            P("dp", "tensor"),
            P("dp", "tensor"),
            P("dp", "tensor"),
            P("tensor", "dp"),
            P("tensor", "dp"),
            P("tensor"),
        ),
        out_specs=P("tensor", "dp"),
        check_vma=False,
    )
```

```python
import functools

import jax
import jax.numpy as jnp
import numpy as np
from jax import lax
from jax.experimental import pallas as pl
from jax.experimental.pallas import tpu as pltpu
from jax.sharding import PartitionSpec as P

FF = 53248
KB = 52
BLK = 32
MESH = pl.DeviceIdType.MESH
BF16 = jnp.bfloat16
F32 = jnp.float32
VMEM_LIMIT = 60 * 1024 * 1024


def paley_table():
    field_square = np.zeros(25, dtype=np.int64)
    for first_part in range(5):
        for second_part in range(5):
            if first_part == 0 and second_part == 0:
                continue
            real_part = (first_part * first_part + 2 * second_part * second_part) % 5
            root_part = 2 * first_part * second_part % 5
            field_square[real_part + 5 * root_part] = 1
    character = np.where(field_square == 1, 1, -1)
    character[0] = 0
    jacobsthal = np.zeros((25, 25), dtype=np.int64)
    for left_item in range(25):
        for right_item in range(25):
            diff_real = (left_item % 5 - right_item % 5) % 5
            diff_root = (left_item // 5 - right_item // 5) % 5
            jacobsthal[left_item, right_item] = character[diff_real + 5 * diff_root]
    conference = np.zeros((26, 26), dtype=np.int64)
    conference[0, 1:] = 1
    conference[1:, 0] = 1
    conference[1:, 1:] = jacobsthal
    outer_part = np.array([[1, -1], [-1, -1]], dtype=np.int64)
    inner_part = np.array([[1, 1], [1, -1]], dtype=np.int64)
    return np.kron(conference, outer_part) + np.kron(np.eye(26, dtype=np.int64), inner_part)


def sylvester_static(order_size):
    position = np.arange(order_size)
    parity = np.zeros((order_size, order_size), dtype=np.int64)
    for bit_place in range(max(order_size.bit_length() - 1, 0)):
        parity = parity + (position[:, None] >> bit_place & position[None, :] >> bit_place & 1)
    return 1 - 2 * (parity & 1)


def inner_table():
    table = np.kron(paley_table(), sylvester_static(BLK))
    order = (4 * np.arange(416)[None, :] + np.arange(4)[:, None]).reshape(-1)
    return table[:, order].astype(np.float32)


def remote(src, dst, send_sem, recv_sem, device):
    return pltpu.make_async_remote_copy(
        src_ref=src, dst_ref=dst, send_sem=send_sem, recv_sem=recv_sem, device_id=device, device_id_type=MESH
    )


def place():
    dp = lax.axis_index("dp")
    t = lax.axis_index("tensor")
    x, yh = lax.div(dp, 2), lax.rem(dp, 2)
    yl, z, core = lax.div(t, 16), lax.rem(lax.div(t, 2), 8), lax.rem(t, 2)
    return dp, t, x, yh, yl, z, core


def unpack(words, scale, j):
    levels = (words & (7 << (3 * j))).astype(F32).astype(BF16) - jnp.asarray(4.0 * 8.0**j, BF16)
    return levels * (scale * 8.0**-j).astype(BF16)


CH = 13
GROUPS = ((0, 2, True, "y"), (2, 3, True, "2"), (5, 4, False, "y"), (9, 4, True, "y"))
EARLY = 2
NC = 4
WC = 512


def kernel(
    tok, gcodes, ucodes, dcodes, gs, us, ds_, flip, table_hbm, out,
    cbuf, ubuf, w, xg, pb, r1, r2, ry, s3, r3, own,
    table, hid, gin, gout, rg, acc, wd,
    qb, rc, rz1, rz, rl,
    ld, sd, as_, bs, ar, br, cr, yr, pr, sr, r1r, r2r, r3r, agr, ccr, zr, yyr,
):
    dp, t, x, yh, yl, z, core = place()
    ho, yo, co = 1 - yh, 1 - yl, 1 - core
    sign = 1 - 2 * core
    tid = lambda a, b, c: a * 16 + b * 2 + c
    zat = lambda k: lax.rem(z + k + 8, 8)
    zsg = lambda k: lax.rem(z + sign * k + 8, 8)
    xr, xl, x2 = lax.rem(x + 1, 4), lax.rem(x + 3, 4), lax.rem(x + 2, 4)
    dev_y, dev_c = (dp, tid(yo, z, core)), (dp, tid(yl, z, co))
    dev_p, dev_s = (dp, tid(yl, zsg(1), core)), (dp, tid(yl, zsg(-1), core))
    dev_u, dev_d = (dp, tid(yl, zat(1), core)), (dp, tid(yl, zat(-1), core))
    dev_r, dev_l, dev_h = (xr * 2 + yh, t), (xl * 2 + yh, t), (x * 2 + ho, t)

    barrier = pltpu.get_barrier_semaphore()
    for device in (dev_r, dev_l, dev_h):
        pl.semaphore_signal(barrier, inc=1, device_id=device, device_id_type=MESH)

    def greet(k, carry):
        pl.semaphore_signal(barrier, inc=1, device_id=(dp, lax.rem(t + k, 32)), device_id_type=MESH)
        return carry

    lax.fori_loop(1, 32, greet, 0)
    gbuf, dbuf = cbuf.at[:, pl.ds(0, 1664)], cbuf.at[pl.ds(0, 416)]
    load_g = pltpu.make_async_copy(gcodes, gbuf, ld.at[0])
    load_u = pltpu.make_async_copy(ucodes, ubuf, ld.at[1])
    load_t = pltpu.make_async_copy(table_hbm, table, ld.at[2])
    load_d = pltpu.make_async_copy(dcodes, dbuf, ld.at[3])
    load_g.start()
    load_u.start()

    apart = lax.broadcasted_iota(jnp.int32, (512, 128), 0) - 4 * lax.broadcasted_iota(jnp.int32, (512, 128), 1)
    pick = jnp.concatenate([jnp.where(apart == j, 1.0, 0.0).astype(BF16) for j in range(4)], axis=1)
    stacked = jnp.concatenate([tok[:, 512 * q : 512 * q + 512] for q in range(4)], axis=0)
    placed = jnp.dot(stacked, pick, preferred_element_type=F32).astype(BF16)
    for q in range(4):
        xg[yl, z, core, :, 512 * q : 512 * q + 512] = placed[16 * q : 16 * q + 16]

    pl.semaphore_wait(barrier, 34)

    sent = [0, 0, 0, 0]

    def size(ref):
        return int(np.prod(ref.shape)) * 2

    def push(phase, src, dst, recv_sem, device, times=1):
        sent[phase] += size(src) * times
        return remote(src, dst, sd.at[phase], recv_sem, device)

    def settle(phase):
        rows = sent[phase] // 512
        for outer in range(1, CH + 1):
            if rows % outer == 0 and rows // outer % 16 == 0 and rows // outer <= 2048:
                span = w.at[pl.ds(0, outer), pl.ds(0, rows // outer)]
                pltpu.make_async_copy(span, span, sd.at[phase]).wait()
                return
        raise ValueError(rows)

    def landed(ref, sem):
        pltpu.make_async_copy(ref, ref, sem).wait()

    yv = (yl, yo)

    def piece(y, back, c, h):
        return xg.at[y, zsg(back), c, :, pl.ds(1024 * h, 1024)]

    def copy_y(y, back, slot, h):
        block = piece(y, back, core, h)
        return block, yr.at[slot, h], dev_y

    def copy_p(k, yy, away, h):
        block = piece(yv[yy], -away, core, h)
        return block, pr.at[k - 1, yy, h], dev_p

    def copy_s(k, yy, away, h):
        block = piece(yv[yy], away, core, h)
        return block, sr.at[k - 1, yy, h], dev_s

    def copy_c(slot, yy, back, h):
        return piece(yv[yy], back, core, h), cr.at[0], dev_c

    def go(copy):
        block, sem, device = copy
        push(0, block, block, sem, device).start()

    def come(copy):
        landed(copy[0], copy[1])

    def dequant(c, carry):
        cols = pl.ds(pl.multiple_of(128 * c, 128), 128)
        for side, (buf, sc) in enumerate(((gbuf, gs), (ubuf, us))):
            scales = sc[:, cols].astype(F32)
            for g in range(16):
                words = buf[32 * g : 32 * g + 32, cols]
                for j in range(4):
                    row = 512 * (g // 4) + 128 * j + 32 * (g % 4)
                    w[c, row : row + 32, 128 * side : 128 * side + 128] = unpack(words, scales[g : g + 1], j)
        return carry

    def ring(k, yy, h, reach_p=4, reach_s=3):
        if k <= reach_p:
            come(copy_p(k, yy, k, h))
            if k < 4:
                go(copy_p(k + 1, yy, k, h))
            if h == 0:
                go(copy_y(yl, -k, k, h))
            go(copy_c(k, yy, -k, h))
        if k <= reach_s:
            come(copy_s(k, yy, k, h))
            if k < 3:
                go(copy_s(k + 1, yy, k, h))
            if h == 0:
                go(copy_y(yl, k, 4 + k, h))
            go(copy_c(4 + k, yy, k, h))

    go(copy_y(yl, 0, 0, 1))
    for h in range(2):
        go(copy_p(1, 0, 0, h))
        go(copy_s(1, 0, 0, h))
    go(copy_y(yl, 0, 0, 0))
    for h in range(2):
        go(copy_c(0, 0, 0, h))
    load_g.wait()
    load_u.wait()
    lax.fori_loop(0, 2, dequant, 0)
    ring(1, 0, 0)
    come(copy_y(yo, 0, 0, 1))
    go(copy_p(1, 1, 0, 1))
    go(copy_s(1, 1, 0, 1))
    ring(1, 0, 1)
    come(copy_y(yo, 0, 0, 0))
    for h in range(2):
        go(copy_c(0, 1, 0, h))
    lax.fori_loop(2, 4, dequant, 0)
    ring(2, 0, 0)
    ring(1, 1, 1)
    ring(2, 0, 1)
    lax.fori_loop(4, 6, dequant, 0)
    ring(3, 0, 0)
    ring(2, 1, 1)
    ring(3, 0, 1)
    lax.fori_loop(6, 9, dequant, 0)
    ring(4, 0, 0)
    ring(3, 1, 1)
    ring(4, 0, 1)
    lax.fori_loop(9, 13, dequant, 0)
    load_t.start()
    load_d.start()
    for back, way, slot in ((-1, 1, 1), (1, 5, 5), (-2, 2, 2), (2, 6, 6), (-3, 3, 3), (3, 7, 7), (-4, 4, 4)):
        come(copy_y(yo, back, way, 0))
        go(copy_c(slot, 1, back, 0))
    ring(4, 1, 1)
    landed(w.at[0], cr.at[0])

    def x_far(c, x_first, times):
        if x_first:
            a, b = pb.at[c, x2, 0], pb.at[c, x2, 1]
            to_a, to_b = r1.at[c, 0], r1.at[c, 1]
        else:
            a, b = pb.at[c, x2, yh, pl.ds(0, 32)], pb.at[c, x2, yh, pl.ds(32, 32)]
            to_a, to_b = r1.at[c, 0, pl.ds(0, 32)], r1.at[c, 1, pl.ds(0, 32)]
        push(1, a, to_a, r1r.at[c], dev_r, times).start()
        push(1, b, to_b, r1r.at[c], dev_l, times).start()

    def x_near(c, x_first, times):
        if x_first:
            a, b, to_a, to_b = pb.at[c, xr], pb.at[c, xl], r2.at[c, 0], r2.at[c, 1]
        else:
            a, b, to_a, to_b = pb.at[c, xr, yh], pb.at[c, xl, yh], r2.at[c, 0, 0], r2.at[c, 1, 0]
        push(1, a, to_a, r2r.at[c], dev_r, times).start()
        push(1, b, to_b, r2r.at[c], dev_l, times).start()

    def add_far(c, x_first, times):
        landed(r1.at[c] if x_first else r1.at[c, 0], r1r.at[c])
        for side, at in ((0, xr), (1, xl)):
            if x_first:
                pb[c, at, side] = (pb[c, at, side].astype(F32) + r1[c, side].astype(F32)).astype(BF16)
            else:
                rows = pl.ds(32 * side, 32)
                pb[c, at, yh, rows] = (
                    pb[c, at, yh, rows].astype(F32) + r1[c, side, 0:32].astype(F32)
                ).astype(BF16)
        x_near(c, x_first, times)

    def multiply(x_first, times, c, carry):
        both = jnp.dot(xg[...].reshape(512, 2048), w[c], preferred_element_type=F32)
        pb[c] = both.astype(BF16).reshape(4, 2, 64, 256)
        if x_first:
            x_far(c, True, times)
        else:
            push(1, pb.at[c, :, ho], ry.at[c], r3r.at[c], dev_h, times).start()
        return carry

    def stage_two(x_first, times, c, carry):
        if x_first:
            add_far(c, True, times)
        else:
            landed(ry.at[c], r3r.at[c])
            for at in range(4):
                pb[c, at, yh] = (pb[c, at, yh].astype(F32) + ry[c, at].astype(F32)).astype(BF16)
            x_far(c, False, times)
        return carry

    def stage_three(x_first, times, c, carry):
        if x_first:
            landed(r2.at[c], r2r.at[c])

            def total(half):
                return pb[c, x, half].astype(F32) + r2[c, 0, half].astype(F32) + r2[c, 1, half].astype(F32)

            s3[c] = total(ho).astype(BF16)
            push(1, s3.at[c], r3.at[c], r3r.at[c], dev_h, times).start()
            own[c] = total(yh)
        else:
            add_far(c, False, times)
        return carry

    def owner(i):
        u = lax.rem(i, 32)
        return 2 * lax.rem(u, 16) + lax.div(u, 16)

    def a2a_out(i):
        slot = lax.div(i, 32)
        return remote(hid.at[i], gin.at[slot, t], as_.at[0], ar.at[slot], (dp, owner(i)))

    def stage_four(x_first, times, c, carry):
        if x_first:
            landed(r3.at[c], r3r.at[c])
            full = own[c] + r3[c].astype(F32)
        else:
            landed(r2.at[c, 0], r2r.at[c])
            full = pb[c, x, yh].astype(F32) + r2[c, 0, 0].astype(F32) + r2[c, 1, 0].astype(F32)
        gate, up = full[:, :128], full[:, 128:]
        signs = flip[pl.ds(pl.multiple_of(128 * c, 128), 128)].reshape(1, 128)
        hidden = (gate / (1.0 + jnp.exp(-gate)) * up).astype(BF16).astype(F32)
        flipped = jnp.where(signs == 1, hidden, -hidden).astype(BF16)
        for h in range(4):
            hid[4 * c + h] = flipped[16 * h : 16 * h + 16]

            @pl.when(owner(4 * c + h) != t)
            def _():
                a2a_out(4 * c + h).start()

        return carry

    mine = 16 * core + lax.div(t, 2)

    def tile(i):
        rows = pl.ds(pl.multiple_of(16 * lax.rem(i, 4), 16), 16)
        return rg.at[dp, rows, pl.ds(pl.multiple_of(128 * lax.div(i, 4), 128), 128)]

    def group_of(i):
        found = 0
        for first, _, _, _ in GROUPS[1:]:
            found = found + jnp.where(i >= 4 * first, 1, 0)
        return found

    def a2a_back(slot, o):
        i = mine + 32 * slot
        return remote(gout.at[slot, o], tile(i), bs.at[slot], br.at[group_of(i)], (dp, o))

    def handle(first, count):
        for slot in range(2):
            i = mine + 32 * slot
            if 32 * slot >= 4 * (first + count) or 32 * slot + 32 <= 4 * first:
                continue

            @pl.when((i >= 4 * first) & (i < 4 * (first + count)))
            def _():
                gin[slot, t] = hid[i]

                landed(gin.at[slot, pl.ds(0, 31)], ar.at[slot])
                values = [gin[slot, g].astype(F32) for g in range(32)]
                for bit in range(5):
                    step = 1 << bit
                    values = [
                        values[g] + values[g + step] if g & step == 0 else values[g - step] - values[g]
                        for g in range(32)
                    ]
                for g in range(32):
                    gout[slot, g] = values[g].astype(BF16)

                def send(k, carry):
                    a2a_back(slot, lax.rem(t + k, 32)).start()
                    return carry

                lax.fori_loop(1, 32, send, 0)
                tile(i)[...] = gout[slot, t]

    def block(g, at, half, rows=slice(0, 64)):
        first, count = GROUPS[g][:2]
        return rg.at[2 * at + half, pl.ds(rows.start, rows.stop - rows.start), pl.ds(128 * first, 128 * count)]

    def blocks(g, n):
        first, count = GROUPS[g][:2]
        return rg.at[pl.ds(0, n), :, pl.ds(128 * first, 128 * count)]

    def spread(g, sem, at, half, device, rows=slice(0, 64)):
        part = block(g, at, half, rows)
        push(2, part, part, agr.at[g, sem], device).start()

    top, low = slice(0, 32), slice(32, 64)

    def gather_one(g):
        first, count, _, kind = GROUPS[g]
        inside = False
        for slot in range(2):
            i = mine + 32 * slot
            inside = inside | ((i >= 4 * first) & (i < 4 * (first + count)))

        @pl.when(inside)
        def _():
            landed(hid.at[pl.ds(0, 4 * count - 1)], br.at[g])

        @pl.when(jnp.logical_not(inside))
        def _():
            landed(hid.at[pl.ds(0, 4 * count)], br.at[g])

        if kind == "x":
            spread(g, 0, x, yh, dev_r)
            spread(g, 1, x, yh, dev_l)
            spread(g, 3, x, yh, dev_h)
        elif kind == "2":
            for sem, device in enumerate((dev_r, dev_l, (x2 * 2 + yh, t), dev_h)):
                spread(g, sem, x, yh, device)
        elif kind == "y":
            spread(g, 0, x, yh, dev_h)
            spread(g, 1, x, yh, dev_r)
            spread(g, 3, x, yh, dev_l)
        else:
            for half in (ho, yh):
                for to in (x2, xr, xl, x):
                    if half is ho or to is not x:
                        spread(g, 3, x, yh, (to * 2 + half, t))

    def gather_two(g):
        if GROUPS[g][3] == "x":
            landed(block(g, xl, yh), agr.at[g, 0])
            spread(g, 2, xl, yh, dev_r, top)
            spread(g, 3, xl, yh, dev_h)
            landed(block(g, xr, yh), agr.at[g, 1])
            spread(g, 2, xr, yh, dev_l, low)
            spread(g, 3, xr, yh, dev_h)
        elif GROUPS[g][3] == "2":
            for sem, at in enumerate((xl, xr, x2)):
                landed(block(g, at, yh), agr.at[g, sem])
                spread(g, 3, at, yh, dev_h)
        else:
            landed(block(g, xl, yh), agr.at[g, 1])
            spread(g, 3, xl, yh, dev_r)
            landed(block(g, x, ho), agr.at[g, 0])
            spread(g, 3, x, ho, dev_r)
            spread(g, 2, x, ho, dev_l)

    def gather_three(g):
        if GROUPS[g][3] == "x":
            landed(block(g, x2, yh), agr.at[g, 2])
            spread(g, 3, x2, yh, dev_h)
        else:
            landed(block(g, xr, ho), agr.at[g, 2])
            spread(g, 3, xr, ho, dev_l)

    def gather_wait(g):
        landed(blocks(g, 7 if GROUPS[g][3] == "d" else 4), agr.at[g, 3])

    def fold(n):
        cols = pl.ds(256 * n, 256)
        for part in range(2):
            rows = pl.ds(832 * part, 832)
            product = jnp.dot(table[rows, :], wd[:, cols], preferred_element_type=F32)
            w[n, rows] = (product * FF**-0.5).astype(BF16)

    def terms_of(first, stop, n):
        units = rg[:, :, 128 * first : 128 * stop].reshape(512, 128 * (stop - first))
        return jnp.dot(units, w[n, pl.ds(128 * first, 128 * (stop - first))], preferred_element_type=F32)

    split = GROUPS[EARLY][0]

    def accumulate():
        for g in range(EARLY):
            gather_wait(g)

        def step(n, carry):
            acc[:, pl.ds(pl.multiple_of(256 * n, 256), 256)] = terms_of(0, split, n)
            return carry

        lax.fori_loop(0, 8, step, 0)

    def dequant_down(c, carry):
        cols = pl.ds(pl.multiple_of(128 * c, 128), 128)
        scales = ds_[:, cols].astype(F32)
        for g in range(13):
            words = dbuf[32 * g : 32 * g + 32, cols]
            for j in range(4):
                row = 416 * j + 32 * g
                wd[row : row + 32, cols] = unpack(words, scales[g : g + 1], j)
        return carry

    def run(stage, g):
        first, count, x_first = GROUPS[g][:3]
        lax.fori_loop(first, first + count, functools.partial(stage, x_first, count), 0)

    def H(g):
        handle(GROUPS[g][0], GROUPS[g][1])

    M, S2, S3, S4 = (functools.partial(run, stage) for stage in (multiply, stage_two, stage_three, stage_four))
    T1, T2, T3, W, A = gather_one, gather_two, gather_three, fold, accumulate

    def unpack_down():
        load_t.wait()
        load_d.wait()
        lax.fori_loop(0, 16, dequant_down, 0)

    M(0), M(3), S2(0), M(2), M(1), S2(3), S3(0)
    unpack_down()
    W(0), W(1), S2(1), W(2), S3(3), S4(0), S2(2), S3(1), S4(3), S3(2), W(3), S4(1), H(0), S4(2), H(3), H(1)
    T1(0), W(4), H(2), T1(3), T2(0), T1(1), T1(2), T2(3), W(5), T3(0), T2(1), W(6), T2(2), T3(3), W(7), T3(2)
    A()

    def pair(c):
        push(3, qb.at[c, co], rc.at[c], ccr.at[c], dev_c, NC).start()

    def z_one(c, times):
        push(3, qb.at[c, core, 0, zat(4)], rz1.at[c, 0], zr.at[0, c], dev_u, times).start()
        push(3, qb.at[c, core, 1, zat(4)], rz1.at[c, 1], zr.at[0, c], dev_d, times).start()
        push(3, qb.at[c, core, yo, z], rl.at[c], yyr.at[c], dev_y, times).start()

    def down(c):
        for part in range(WC // 256):
            n = WC // 256 * c + part
            cols = pl.ds(pl.multiple_of(256 * n, 256), 256)
            terms = (acc[:, cols] + terms_of(split, CH, n)).astype(BF16)
            for cc in range(2):
                for yy in range(2):
                    for zz in range(8):
                        row = 16 * (16 * yy + 2 * zz + cc)
                        qb[c, cc, yy, zz, :, 256 * part : 256 * part + 256] = terms[row : row + 16]
        pair(c)

    def after_pair(times, c):
        landed(rc.at[c], ccr.at[c])
        qb[c, core] = (qb[c, core].astype(F32) + rc[c].astype(F32)).astype(BF16)
        z_one(c, times)

    def z_round(r, c, carry):
        landed(rz1.at[c] if r == 2 else rz.at[r - 3, c], zr.at[r - 2, c])
        for side in range(2):
            at = zat((5 - r) * (1 - 2 * side))
            if r == 2:
                qb[c, core, side, at] = (qb[c, core, side, at].astype(F32) + rz1[c, side].astype(F32)).astype(BF16)
            else:
                for yy in range(2):
                    qb[c, core, yy, at] = (
                        qb[c, core, yy, at].astype(F32) + rz[r - 3, c, side, yy].astype(F32)
                    ).astype(BF16)
            if r < 4:
                push(3, qb.at[c, core, :, at], rz.at[r - 2, c, side], zr.at[r - 1, c], (dev_u, dev_d)[side], NC).start()
            else:
                for row, to in ((0, yl), (1, yo)):
                    device = (dp, tid(to, at, core))
                    push(3, qb.at[c, core, to, at], rz.at[2, c, side, row], zr.at[3, c], device, NC).start()
        return carry

    def finish(c, carry):
        landed(rl.at[c], yyr.at[c])
        landed(rz.at[2, c], zr.at[3, c])
        total = qb[c, core, yl, z].astype(F32) + rl[c].astype(F32)
        for side in range(2):
            for row in range(2):
                total = total + rz[2, c, side, row].astype(F32)
        cols = pl.ds(pl.multiple_of(WC * c, WC), WC)
        out[:, cols] = total.astype(BF16)
        return carry

    for g in range(EARLY, len(GROUPS)):
        gather_wait(g)

    def start(c, carry):
        down(c)

        @pl.when(c > 0)
        def _():
            after_pair(NC - 1, c - 1)

        return carry

    lax.fori_loop(0, NC, start, 0)
    after_pair(1, NC - 1)
    for step in (functools.partial(z_round, 2), functools.partial(z_round, 3), functools.partial(z_round, 4), finish):
        lax.fori_loop(0, NC, step, 0)

    for phase in range(4):
        settle(phase)
    for slot in range(2):
        i = mine + 32 * slot

        @pl.when(i < 4 * CH)
        def _():
            landed(gout.at[slot, pl.ds(0, 31)], bs.at[slot])

    two = mine + 32 < 4 * CH

    @pl.when(two)
    def _():
        landed(hid.at[pl.ds(0, 4 * CH - 2)], as_.at[0])

    @pl.when(jnp.logical_not(two))
    def _():
        landed(hid.at[pl.ds(0, 4 * CH - 1)], as_.at[0])


def per_device(
    tokens, gate_codes, gate_scales, up_codes, up_scales, down_codes, down_scales, flip_signs
):
    vm = pl.BlockSpec(memory_space=pltpu.VMEM)
    hbm = pl.BlockSpec(memory_space=pl.ANY)
    dma = pltpu.SemaphoreType.DMA
    ng = len(GROUPS)
    return pl.pallas_call(
        kernel,
        out_shape=jax.ShapeDtypeStruct((16, 2048), BF16),
        in_specs=[vm, hbm, hbm, hbm, vm, vm, vm, vm, hbm],
        out_specs=vm,
        scratch_shapes=[
            pltpu.VMEM((512, 2048), jnp.int32),
            pltpu.VMEM((512, 1664), jnp.int32),
            pltpu.VMEM((CH, 2048, 256), BF16),
            pltpu.VMEM((2, 8, 2, 16, 2048), BF16),
            pltpu.VMEM((CH, 4, 2, 64, 256), BF16),
            pltpu.VMEM((CH, 2, 64, 256), BF16),
            pltpu.VMEM((CH, 2, 2, 64, 256), BF16),
            pltpu.VMEM((CH, 4, 64, 256), BF16),
            pltpu.VMEM((CH, 64, 256), BF16),
            pltpu.VMEM((CH, 64, 256), BF16),
            pltpu.VMEM((CH, 64, 256), F32),
            pltpu.VMEM((1664, 1664), BF16),
            pltpu.VMEM((4 * CH, 16, 128), BF16),
            pltpu.VMEM((2, 32, 16, 128), BF16),
            pltpu.VMEM((2, 32, 16, 128), BF16),
            pltpu.VMEM((8, 64, 1664), BF16),
            pltpu.VMEM((512, 2048), F32),
            pltpu.VMEM((1664, 2048), BF16),
            pltpu.VMEM((NC, 2, 2, 8, 16, WC), BF16),
            pltpu.VMEM((NC, 2, 8, 16, WC), BF16),
            pltpu.VMEM((NC, 2, 16, WC), BF16),
            pltpu.VMEM((3, NC, 2, 2, 16, WC), BF16),
            pltpu.VMEM((NC, 16, WC), BF16),
            dma((4,)), dma((4,)), dma((1,)), dma((2,)), dma((2,)), dma((ng,)), dma((1,)),
            dma((8, 2)), dma((4, 2, 2)), dma((3, 2, 2)), dma((CH,)), dma((CH,)), dma((CH,)), dma((ng, 4)),
            dma((NC,)), dma((4, NC)), dma((NC,)),
        ],
        compiler_params=pltpu.CompilerParams(
            collective_id=0, has_side_effects=True, vmem_limit_bytes=VMEM_LIMIT
        ),
        cost_estimate=pl.CostEstimate(flops=14 * 10**9, bytes_accessed=2 * 10**7, transcendentals=10**5),
    )(
        tokens, gate_codes, up_codes, down_codes, gate_scales, up_scales, down_scales,
        flip_signs, jnp.asarray(inner_table(), dtype=BF16),
    )


def solution(mesh):
    return jax.shard_map(
        per_device,
        mesh=mesh,
        in_specs=(
            P("tensor", "dp"),
            P("dp", "tensor"),
            P("dp", "tensor"),
            P("dp", "tensor"),
            P("dp", "tensor"),
            P("tensor", "dp"),
            P("tensor", "dp"),
            P("tensor"),
        ),
        out_specs=P("tensor", "dp"),
        check_vma=False,
    )
```

```python
import functools

import jax
import jax.numpy as jnp
import numpy as np
from jax import lax
from jax.experimental import pallas as pl
from jax.experimental.pallas import tpu as pltpu
from jax.sharding import PartitionSpec as P

FF = 53248
KB = 52
BLK = 32
MESH = pl.DeviceIdType.MESH
BF16 = jnp.bfloat16
F32 = jnp.float32
VMEM_LIMIT = 60 * 1024 * 1024


def paley_table():
    field_square = np.zeros(25, dtype=np.int64)
    for first_part in range(5):
        for second_part in range(5):
            if first_part == 0 and second_part == 0:
                continue
            real_part = (first_part * first_part + 2 * second_part * second_part) % 5
            root_part = 2 * first_part * second_part % 5
            field_square[real_part + 5 * root_part] = 1
    character = np.where(field_square == 1, 1, -1)
    character[0] = 0
    jacobsthal = np.zeros((25, 25), dtype=np.int64)
    for left_item in range(25):
        for right_item in range(25):
            diff_real = (left_item % 5 - right_item % 5) % 5
            diff_root = (left_item // 5 - right_item // 5) % 5
            jacobsthal[left_item, right_item] = character[diff_real + 5 * diff_root]
    conference = np.zeros((26, 26), dtype=np.int64)
    conference[0, 1:] = 1
    conference[1:, 0] = 1
    conference[1:, 1:] = jacobsthal
    outer_part = np.array([[1, -1], [-1, -1]], dtype=np.int64)
    inner_part = np.array([[1, 1], [1, -1]], dtype=np.int64)
    return np.kron(conference, outer_part) + np.kron(np.eye(26, dtype=np.int64), inner_part)


def sylvester_static(order_size):
    position = np.arange(order_size)
    parity = np.zeros((order_size, order_size), dtype=np.int64)
    for bit_place in range(max(order_size.bit_length() - 1, 0)):
        parity = parity + (position[:, None] >> bit_place & position[None, :] >> bit_place & 1)
    return 1 - 2 * (parity & 1)


def inner_table():
    table = np.kron(paley_table(), sylvester_static(BLK))
    order = (4 * np.arange(416)[None, :] + np.arange(4)[:, None]).reshape(-1)
    return table[:, order].astype(np.float32)


def remote(src, dst, send_sem, recv_sem, device):
    return pltpu.make_async_remote_copy(
        src_ref=src, dst_ref=dst, send_sem=send_sem, recv_sem=recv_sem, device_id=device, device_id_type=MESH
    )


def place():
    dp = lax.axis_index("dp")
    t = lax.axis_index("tensor")
    x, yh = lax.div(dp, 2), lax.rem(dp, 2)
    yl, z, core = lax.div(t, 16), lax.rem(lax.div(t, 2), 8), lax.rem(t, 2)
    return dp, t, x, yh, yl, z, core


def unpack(words, scale, j):
    levels = (words & (7 << (3 * j))).astype(F32).astype(BF16) - jnp.asarray(4.0 * 8.0**j, BF16)
    return levels * (scale * 8.0**-j).astype(BF16)


CH = 13
GROUPS = ((0, 2, True, "y"), (2, 3, True, "2"), (5, 4, False, "y"), (9, 4, True, "y"))
EARLY = 2
NC = 4
WC = 512


def kernel(
    tok, gcodes, ucodes, dcodes, gs, us, ds_, flip, table_hbm, out,
    cbuf, ubuf, w, xg, pb, r1, r2, ry, s3, r3, own,
    table, hid, gin, gout, rg, acc, wd,
    qb, rc, rz1, rz, rl,
    ld, sd, as_, bs, ar, br, cr, yr, pr, sr, r1r, r2r, r3r, agr, ccr, zr, yyr,
):
    dp, t, x, yh, yl, z, core = place()
    ho, yo, co = 1 - yh, 1 - yl, 1 - core
    sign = 1 - 2 * core
    tid = lambda a, b, c: a * 16 + b * 2 + c
    zat = lambda k: lax.rem(z + k + 8, 8)
    zsg = lambda k: lax.rem(z + sign * k + 8, 8)
    xr, xl, x2 = lax.rem(x + 1, 4), lax.rem(x + 3, 4), lax.rem(x + 2, 4)
    dev_y, dev_c = (dp, tid(yo, z, core)), (dp, tid(yl, z, co))
    dev_p, dev_s = (dp, tid(yl, zsg(1), core)), (dp, tid(yl, zsg(-1), core))
    dev_u, dev_d = (dp, tid(yl, zat(1), core)), (dp, tid(yl, zat(-1), core))
    dev_r, dev_l, dev_h = (xr * 2 + yh, t), (xl * 2 + yh, t), (x * 2 + ho, t)

    barrier = pltpu.get_barrier_semaphore()
    for device in (dev_r, dev_l, dev_h, dev_y, dev_c, dev_p, dev_s):
        pl.semaphore_signal(barrier, inc=1, device_id=device, device_id_type=MESH)
    gbuf, dbuf = cbuf.at[:, pl.ds(0, 1664)], cbuf.at[pl.ds(0, 416)]
    load_g = pltpu.make_async_copy(gcodes, gbuf, ld.at[0])
    load_u = pltpu.make_async_copy(ucodes, ubuf, ld.at[1])
    load_t = pltpu.make_async_copy(table_hbm, table, ld.at[2])
    load_d = pltpu.make_async_copy(dcodes, dbuf, ld.at[3])
    load_g.start()
    load_u.start()

    apart = lax.broadcasted_iota(jnp.int32, (512, 128), 0) - 4 * lax.broadcasted_iota(jnp.int32, (512, 128), 1)
    pick = jnp.concatenate([jnp.where(apart == j, 1.0, 0.0).astype(BF16) for j in range(4)], axis=1)
    stacked = jnp.concatenate([tok[:, 512 * q : 512 * q + 512] for q in range(4)], axis=0)
    placed = jnp.dot(stacked, pick, preferred_element_type=F32).astype(BF16)
    for q in range(4):
        xg[yl, z, core, :, 512 * q : 512 * q + 512] = placed[16 * q : 16 * q + 16]

    pl.semaphore_wait(barrier, 7)

    sent = [0, 0, 0, 0]

    def size(ref):
        return int(np.prod(ref.shape)) * 2

    def push(phase, src, dst, recv_sem, device, times=1):
        sent[phase] += size(src) * times
        return remote(src, dst, sd.at[phase], recv_sem, device)

    def settle(phase):
        rows = sent[phase] // 512
        for outer in range(1, CH + 1):
            if rows % outer == 0 and rows // outer % 16 == 0 and rows // outer <= 2048:
                span = w.at[pl.ds(0, outer), pl.ds(0, rows // outer)]
                pltpu.make_async_copy(span, span, sd.at[phase]).wait()
                return
        raise ValueError(rows)

    def landed(ref, sem):
        pltpu.make_async_copy(ref, ref, sem).wait()

    yv = (yl, yo)

    def piece(y, back, c, h):
        return xg.at[y, zsg(back), c, :, pl.ds(1024 * h, 1024)]

    def copy_y(y, back, slot, h):
        block = piece(y, back, core, h)
        return block, yr.at[slot, h], dev_y

    def copy_p(k, yy, away, h):
        block = piece(yv[yy], -away, core, h)
        return block, pr.at[k - 1, yy, h], dev_p

    def copy_s(k, yy, away, h):
        block = piece(yv[yy], away, core, h)
        return block, sr.at[k - 1, yy, h], dev_s

    def copy_c(slot, yy, back, h):
        return piece(yv[yy], back, core, h), cr.at[0], dev_c

    def go(copy):
        block, sem, device = copy
        push(0, block, block, sem, device).start()

    def come(copy):
        landed(copy[0], copy[1])

    def dequant(c, carry):
        cols = pl.ds(pl.multiple_of(128 * c, 128), 128)
        for side, (buf, sc) in enumerate(((gbuf, gs), (ubuf, us))):
            scales = sc[:, cols].astype(F32)
            for g in range(16):
                words = buf[32 * g : 32 * g + 32, cols]
                for j in range(4):
                    row = 512 * (g // 4) + 128 * j + 32 * (g % 4)
                    w[c, row : row + 32, 128 * side : 128 * side + 128] = unpack(words, scales[g : g + 1], j)
        return carry

    def ring(k, yy, h, reach_p=4, reach_s=3):
        if k <= reach_p:
            come(copy_p(k, yy, k, h))
            if k < 4:
                go(copy_p(k + 1, yy, k, h))
            if h == 0:
                go(copy_y(yl, -k, k, h))
            go(copy_c(k, yy, -k, h))
        if k <= reach_s:
            come(copy_s(k, yy, k, h))
            if k < 3:
                go(copy_s(k + 1, yy, k, h))
            if h == 0:
                go(copy_y(yl, k, 4 + k, h))
            go(copy_c(4 + k, yy, k, h))

    go(copy_y(yl, 0, 0, 1))
    for h in range(2):
        go(copy_p(1, 0, 0, h))
        go(copy_s(1, 0, 0, h))
    go(copy_y(yl, 0, 0, 0))
    for h in range(2):
        go(copy_c(0, 0, 0, h))
    load_g.wait()
    load_u.wait()
    lax.fori_loop(0, 2, dequant, 0)
    ring(1, 0, 0)
    come(copy_y(yo, 0, 0, 1))
    go(copy_p(1, 1, 0, 1))
    go(copy_s(1, 1, 0, 1))
    ring(1, 0, 1)
    come(copy_y(yo, 0, 0, 0))
    for h in range(2):
        go(copy_c(0, 1, 0, h))
    lax.fori_loop(2, 4, dequant, 0)
    ring(2, 0, 0)
    ring(1, 1, 1)
    ring(2, 0, 1)
    lax.fori_loop(4, 6, dequant, 0)
    ring(3, 0, 0)
    ring(2, 1, 1)
    ring(3, 0, 1)
    lax.fori_loop(6, 9, dequant, 0)
    ring(4, 0, 0)
    ring(3, 1, 1)
    ring(4, 0, 1)
    lax.fori_loop(9, 13, dequant, 0)
    load_t.start()
    load_d.start()
    for back, way, slot in ((-1, 1, 1), (1, 5, 5), (-2, 2, 2), (2, 6, 6), (-3, 3, 3), (3, 7, 7), (-4, 4, 4)):
        come(copy_y(yo, back, way, 0))
        go(copy_c(slot, 1, back, 0))
    ring(4, 1, 1)
    landed(w.at[0], cr.at[0])

    def x_far(c, x_first, times):
        if x_first:
            a, b = pb.at[c, x2, 0], pb.at[c, x2, 1]
            to_a, to_b = r1.at[c, 0], r1.at[c, 1]
        else:
            a, b = pb.at[c, x2, yh, pl.ds(0, 32)], pb.at[c, x2, yh, pl.ds(32, 32)]
            to_a, to_b = r1.at[c, 0, pl.ds(0, 32)], r1.at[c, 1, pl.ds(0, 32)]
        push(1, a, to_a, r1r.at[c], dev_r, times).start()
        push(1, b, to_b, r1r.at[c], dev_l, times).start()

    def x_near(c, x_first, times):
        if x_first:
            a, b, to_a, to_b = pb.at[c, xr], pb.at[c, xl], r2.at[c, 0], r2.at[c, 1]
        else:
            a, b, to_a, to_b = pb.at[c, xr, yh], pb.at[c, xl, yh], r2.at[c, 0, 0], r2.at[c, 1, 0]
        push(1, a, to_a, r2r.at[c], dev_r, times).start()
        push(1, b, to_b, r2r.at[c], dev_l, times).start()

    def add_far(c, x_first, times):
        landed(r1.at[c] if x_first else r1.at[c, 0], r1r.at[c])
        for side, at in ((0, xr), (1, xl)):
            if x_first:
                pb[c, at, side] = (pb[c, at, side].astype(F32) + r1[c, side].astype(F32)).astype(BF16)
            else:
                rows = pl.ds(32 * side, 32)
                pb[c, at, yh, rows] = (
                    pb[c, at, yh, rows].astype(F32) + r1[c, side, 0:32].astype(F32)
                ).astype(BF16)
        x_near(c, x_first, times)

    def multiply(x_first, times, c, carry):
        both = jnp.dot(xg[...].reshape(512, 2048), w[c], preferred_element_type=F32)
        pb[c] = both.astype(BF16).reshape(4, 2, 64, 256)
        if x_first:
            x_far(c, True, times)
        else:
            push(1, pb.at[c, :, ho], ry.at[c], r3r.at[c], dev_h, times).start()
        return carry

    def stage_two(x_first, times, c, carry):
        if x_first:
            add_far(c, True, times)
        else:
            landed(ry.at[c], r3r.at[c])
            for at in range(4):
                pb[c, at, yh] = (pb[c, at, yh].astype(F32) + ry[c, at].astype(F32)).astype(BF16)
            x_far(c, False, times)
        return carry

    def stage_three(x_first, times, c, carry):
        if x_first:
            landed(r2.at[c], r2r.at[c])

            def total(half):
                return pb[c, x, half].astype(F32) + r2[c, 0, half].astype(F32) + r2[c, 1, half].astype(F32)

            s3[c] = total(ho).astype(BF16)
            push(1, s3.at[c], r3.at[c], r3r.at[c], dev_h, times).start()
            own[c] = total(yh)
        else:
            add_far(c, False, times)
        return carry

    def owner(i):
        u = lax.rem(i, 32)
        return 2 * lax.rem(u, 16) + lax.div(u, 16)

    def a2a_out(i):
        slot = lax.div(i, 32)
        return remote(hid.at[i], gin.at[slot, t], as_.at[0], ar.at[slot], (dp, owner(i)))

    def stage_four(x_first, times, c, carry):
        if x_first:
            landed(r3.at[c], r3r.at[c])
            full = own[c] + r3[c].astype(F32)
        else:
            landed(r2.at[c, 0], r2r.at[c])
            full = pb[c, x, yh].astype(F32) + r2[c, 0, 0].astype(F32) + r2[c, 1, 0].astype(F32)
        gate, up = full[:, :128], full[:, 128:]
        signs = flip[pl.ds(pl.multiple_of(128 * c, 128), 128)].reshape(1, 128)
        hidden = (gate / (1.0 + jnp.exp(-gate)) * up).astype(BF16).astype(F32)
        flipped = jnp.where(signs == 1, hidden, -hidden).astype(BF16)
        for h in range(4):
            hid[4 * c + h] = flipped[16 * h : 16 * h + 16]

            @pl.when(owner(4 * c + h) != t)
            def _():
                a2a_out(4 * c + h).start()

        return carry

    mine = 16 * core + lax.div(t, 2)

    def tile(i):
        rows = pl.ds(pl.multiple_of(16 * lax.rem(i, 4), 16), 16)
        return rg.at[dp, rows, pl.ds(pl.multiple_of(128 * lax.div(i, 4), 128), 128)]

    def group_of(i):
        found = 0
        for first, _, _, _ in GROUPS[1:]:
            found = found + jnp.where(i >= 4 * first, 1, 0)
        return found

    def a2a_back(slot, o):
        i = mine + 32 * slot
        return remote(gout.at[slot, o], tile(i), bs.at[slot], br.at[group_of(i)], (dp, o))

    def handle(first, count):
        for slot in range(2):
            i = mine + 32 * slot
            if 32 * slot >= 4 * (first + count) or 32 * slot + 32 <= 4 * first:
                continue

            @pl.when((i >= 4 * first) & (i < 4 * (first + count)))
            def _():
                gin[slot, t] = hid[i]

                landed(gin.at[slot, pl.ds(0, 31)], ar.at[slot])
                values = [gin[slot, g].astype(F32) for g in range(32)]
                for bit in range(5):
                    step = 1 << bit
                    values = [
                        values[g] + values[g + step] if g & step == 0 else values[g - step] - values[g]
                        for g in range(32)
                    ]
                for g in range(32):
                    gout[slot, g] = values[g].astype(BF16)

                def send(k, carry):
                    a2a_back(slot, lax.rem(t + k, 32)).start()
                    return carry

                lax.fori_loop(1, 32, send, 0)
                tile(i)[...] = gout[slot, t]

    def block(g, at, half, rows=slice(0, 64)):
        first, count = GROUPS[g][:2]
        return rg.at[2 * at + half, pl.ds(rows.start, rows.stop - rows.start), pl.ds(128 * first, 128 * count)]

    def blocks(g, n):
        first, count = GROUPS[g][:2]
        return rg.at[pl.ds(0, n), :, pl.ds(128 * first, 128 * count)]

    def spread(g, sem, at, half, device, rows=slice(0, 64)):
        part = block(g, at, half, rows)
        push(2, part, part, agr.at[g, sem], device).start()

    top, low = slice(0, 32), slice(32, 64)

    def gather_one(g):
        first, count, _, kind = GROUPS[g]
        inside = False
        for slot in range(2):
            i = mine + 32 * slot
            inside = inside | ((i >= 4 * first) & (i < 4 * (first + count)))

        @pl.when(inside)
        def _():
            landed(hid.at[pl.ds(0, 4 * count - 1)], br.at[g])

        @pl.when(jnp.logical_not(inside))
        def _():
            landed(hid.at[pl.ds(0, 4 * count)], br.at[g])

        if kind == "x":
            spread(g, 0, x, yh, dev_r)
            spread(g, 1, x, yh, dev_l)
            spread(g, 3, x, yh, dev_h)
        elif kind == "2":
            for sem, device in enumerate((dev_r, dev_l, (x2 * 2 + yh, t), dev_h)):
                spread(g, sem, x, yh, device)
        elif kind == "y":
            spread(g, 0, x, yh, dev_h)
            spread(g, 1, x, yh, dev_r)
            spread(g, 3, x, yh, dev_l)
        else:
            for half in (ho, yh):
                for to in (x2, xr, xl, x):
                    if half is ho or to is not x:
                        spread(g, 3, x, yh, (to * 2 + half, t))

    def gather_two(g):
        if GROUPS[g][3] == "x":
            landed(block(g, xl, yh), agr.at[g, 0])
            spread(g, 2, xl, yh, dev_r, top)
            spread(g, 3, xl, yh, dev_h)
            landed(block(g, xr, yh), agr.at[g, 1])
            spread(g, 2, xr, yh, dev_l, low)
            spread(g, 3, xr, yh, dev_h)
        elif GROUPS[g][3] == "2":
            for sem, at in enumerate((xl, xr, x2)):
                landed(block(g, at, yh), agr.at[g, sem])
                spread(g, 3, at, yh, dev_h)
        else:
            landed(block(g, xl, yh), agr.at[g, 1])
            spread(g, 3, xl, yh, dev_r)
            landed(block(g, x, ho), agr.at[g, 0])
            spread(g, 3, x, ho, dev_r)
            spread(g, 2, x, ho, dev_l)

    def gather_three(g):
        if GROUPS[g][3] == "x":
            landed(block(g, x2, yh), agr.at[g, 2])
            spread(g, 3, x2, yh, dev_h)
        else:
            landed(block(g, xr, ho), agr.at[g, 2])
            spread(g, 3, xr, ho, dev_l)

    def gather_wait(g):
        landed(blocks(g, 7 if GROUPS[g][3] == "d" else 4), agr.at[g, 3])

    def fold(n):
        cols = pl.ds(256 * n, 256)
        for part in range(2):
            rows = pl.ds(832 * part, 832)
            product = jnp.dot(table[rows, :], wd[:, cols], preferred_element_type=F32)
            w[n, rows] = (product * FF**-0.5).astype(BF16)

    def terms_of(first, stop, n):
        units = rg[:, :, 128 * first : 128 * stop].reshape(512, 128 * (stop - first))
        return jnp.dot(units, w[n, pl.ds(128 * first, 128 * (stop - first))], preferred_element_type=F32)

    split = GROUPS[EARLY][0]

    def accumulate():
        for g in range(EARLY):
            gather_wait(g)

        def step(n, carry):
            acc[:, pl.ds(pl.multiple_of(256 * n, 256), 256)] = terms_of(0, split, n)
            return carry

        lax.fori_loop(0, 8, step, 0)

    def dequant_down(c, carry):
        cols = pl.ds(pl.multiple_of(128 * c, 128), 128)
        scales = ds_[:, cols].astype(F32)
        for g in range(13):
            words = dbuf[32 * g : 32 * g + 32, cols]
            for j in range(4):
                row = 416 * j + 32 * g
                wd[row : row + 32, cols] = unpack(words, scales[g : g + 1], j)
        return carry

    def run(stage, g):
        first, count, x_first = GROUPS[g][:3]
        lax.fori_loop(first, first + count, functools.partial(stage, x_first, count), 0)

    def H(g):
        handle(GROUPS[g][0], GROUPS[g][1])

    M, S2, S3, S4 = (functools.partial(run, stage) for stage in (multiply, stage_two, stage_three, stage_four))
    T1, T2, T3, W, A = gather_one, gather_two, gather_three, fold, accumulate

    def unpack_down():
        load_t.wait()
        load_d.wait()
        lax.fori_loop(0, 16, dequant_down, 0)

    M(0), M(3), S2(0), M(2), M(1), S2(3), S3(0)
    unpack_down()
    W(0), W(1), S2(1), W(2), S3(3), S4(0), S2(2), S3(1), S4(3), S3(2), W(3), S4(1), H(0), S4(2), H(3), H(1)
    T1(0), W(4), H(2), T1(3), T2(0), T1(1), T1(2), T2(3), W(5), T3(0), T2(1), W(6), T2(2), T3(3), W(7), T3(2)
    A()

    def pair(c):
        push(3, qb.at[c, co], rc.at[c], ccr.at[c], dev_c, NC).start()

    def z_one(c, times):
        push(3, qb.at[c, core, 0, zat(4)], rz1.at[c, 0], zr.at[0, c], dev_u, times).start()
        push(3, qb.at[c, core, 1, zat(4)], rz1.at[c, 1], zr.at[0, c], dev_d, times).start()
        push(3, qb.at[c, core, yo, z], rl.at[c], yyr.at[c], dev_y, times).start()

    def down(c):
        for part in range(WC // 256):
            n = WC // 256 * c + part
            cols = pl.ds(pl.multiple_of(256 * n, 256), 256)
            terms = (acc[:, cols] + terms_of(split, CH, n)).astype(BF16)
            for cc in range(2):
                for yy in range(2):
                    for zz in range(8):
                        row = 16 * (16 * yy + 2 * zz + cc)
                        qb[c, cc, yy, zz, :, 256 * part : 256 * part + 256] = terms[row : row + 16]
        pair(c)

    def after_pair(times, c):
        landed(rc.at[c], ccr.at[c])
        qb[c, core] = (qb[c, core].astype(F32) + rc[c].astype(F32)).astype(BF16)
        z_one(c, times)

    def z_round(r, c, carry):
        landed(rz1.at[c] if r == 2 else rz.at[r - 3, c], zr.at[r - 2, c])
        for side in range(2):
            at = zat((5 - r) * (1 - 2 * side))
            if r == 2:
                qb[c, core, side, at] = (qb[c, core, side, at].astype(F32) + rz1[c, side].astype(F32)).astype(BF16)
            else:
                for yy in range(2):
                    qb[c, core, yy, at] = (
                        qb[c, core, yy, at].astype(F32) + rz[r - 3, c, side, yy].astype(F32)
                    ).astype(BF16)
            if r < 4:
                push(3, qb.at[c, core, :, at], rz.at[r - 2, c, side], zr.at[r - 1, c], (dev_u, dev_d)[side], NC).start()
            else:
                for row, to in ((0, yl), (1, yo)):
                    device = (dp, tid(to, at, core))
                    push(3, qb.at[c, core, to, at], rz.at[2, c, side, row], zr.at[3, c], device, NC).start()
        return carry

    def finish(c, carry):
        landed(rl.at[c], yyr.at[c])
        landed(rz.at[2, c], zr.at[3, c])
        total = qb[c, core, yl, z].astype(F32) + rl[c].astype(F32)
        for side in range(2):
            for row in range(2):
                total = total + rz[2, c, side, row].astype(F32)
        cols = pl.ds(pl.multiple_of(WC * c, WC), WC)
        out[:, cols] = total.astype(BF16)
        return carry

    for g in range(EARLY, len(GROUPS)):
        gather_wait(g)

    def start(c, carry):
        down(c)

        @pl.when(c > 0)
        def _():
            after_pair(NC - 1, c - 1)

        return carry

    lax.fori_loop(0, NC, start, 0)
    after_pair(1, NC - 1)
    for step in (functools.partial(z_round, 2), functools.partial(z_round, 3), functools.partial(z_round, 4), finish):
        lax.fori_loop(0, NC, step, 0)

    for phase in range(4):
        settle(phase)
    for slot in range(2):
        i = mine + 32 * slot

        @pl.when(i < 4 * CH)
        def _():
            landed(gout.at[slot, pl.ds(0, 31)], bs.at[slot])

    two = mine + 32 < 4 * CH

    @pl.when(two)
    def _():
        landed(hid.at[pl.ds(0, 4 * CH - 2)], as_.at[0])

    @pl.when(jnp.logical_not(two))
    def _():
        landed(hid.at[pl.ds(0, 4 * CH - 1)], as_.at[0])


def per_device(
    tokens, gate_codes, gate_scales, up_codes, up_scales, down_codes, down_scales, flip_signs
):
    vm = pl.BlockSpec(memory_space=pltpu.VMEM)
    hbm = pl.BlockSpec(memory_space=pl.ANY)
    dma = pltpu.SemaphoreType.DMA
    ng = len(GROUPS)
    return pl.pallas_call(
        kernel,
        out_shape=jax.ShapeDtypeStruct((16, 2048), BF16),
        in_specs=[vm, hbm, hbm, hbm, vm, vm, vm, vm, hbm],
        out_specs=vm,
        scratch_shapes=[
            pltpu.VMEM((512, 2048), jnp.int32),
            pltpu.VMEM((512, 1664), jnp.int32),
            pltpu.VMEM((CH, 2048, 256), BF16),
            pltpu.VMEM((2, 8, 2, 16, 2048), BF16),
            pltpu.VMEM((CH, 4, 2, 64, 256), BF16),
            pltpu.VMEM((CH, 2, 64, 256), BF16),
            pltpu.VMEM((CH, 2, 2, 64, 256), BF16),
            pltpu.VMEM((CH, 4, 64, 256), BF16),
            pltpu.VMEM((CH, 64, 256), BF16),
            pltpu.VMEM((CH, 64, 256), BF16),
            pltpu.VMEM((CH, 64, 256), F32),
            pltpu.VMEM((1664, 1664), BF16),
            pltpu.VMEM((4 * CH, 16, 128), BF16),
            pltpu.VMEM((2, 32, 16, 128), BF16),
            pltpu.VMEM((2, 32, 16, 128), BF16),
            pltpu.VMEM((8, 64, 1664), BF16),
            pltpu.VMEM((512, 2048), F32),
            pltpu.VMEM((1664, 2048), BF16),
            pltpu.VMEM((NC, 2, 2, 8, 16, WC), BF16),
            pltpu.VMEM((NC, 2, 8, 16, WC), BF16),
            pltpu.VMEM((NC, 2, 16, WC), BF16),
            pltpu.VMEM((3, NC, 2, 2, 16, WC), BF16),
            pltpu.VMEM((NC, 16, WC), BF16),
            dma((4,)), dma((4,)), dma((1,)), dma((2,)), dma((2,)), dma((ng,)), dma((1,)),
            dma((8, 2)), dma((4, 2, 2)), dma((3, 2, 2)), dma((CH,)), dma((CH,)), dma((CH,)), dma((ng, 4)),
            dma((NC,)), dma((4, NC)), dma((NC,)),
        ],
        compiler_params=pltpu.CompilerParams(
            collective_id=0, has_side_effects=True, vmem_limit_bytes=VMEM_LIMIT
        ),
        cost_estimate=pl.CostEstimate(flops=14 * 10**9, bytes_accessed=2 * 10**7, transcendentals=10**5),
    )(
        tokens, gate_codes, up_codes, down_codes, gate_scales, up_scales, down_scales,
        flip_signs, jnp.asarray(inner_table(), dtype=BF16),
    )


def solution(mesh):
    return jax.shard_map(
        per_device,
        mesh=mesh,
        in_specs=(
            P("tensor", "dp"),
            P("dp", "tensor"),
            P("dp", "tensor"),
            P("dp", "tensor"),
            P("dp", "tensor"),
            P("tensor", "dp"),
            P("tensor", "dp"),
            P("tensor"),
        ),
        out_specs=P("tensor", "dp"),
        check_vma=False,
    )
```
